256 devices in a mesh: seq: 32 (over x, y, core), head: 8 (over z).
Axes of the slice: x: 4, y: 4, z: 8, core: 2. Of those that a mesh axis runs over, the one named last changes fastest.
Arguments:
- residual: bfloat16 [16384, 4096], P(('seq', 'head')), may hold values from -6 to 6
- sliding_query_heads: bfloat16 [16384, 4096], P('seq', 'head'), may hold values from -64 to 64
- sliding_key_heads: bfloat16 [16384, 1024], P('seq', 'head'), may hold values from -6 to 6
- sliding_value_heads: bfloat16 [16384, 1024], P('seq', 'head'), may hold values from -6 to 6
- output_weight: bfloat16 [4096, 4096], P('head'), may hold values from -0.5 to 0.5
- norm_gain: float32 [4096], replicated, may hold values from 0.5 to 1.5
- query_weight: bfloat16 [4096, 1024], P(None, 'head'), may hold values from -0.09375 to 0.09375
- key_weight: bfloat16 [4096, 1024], P(None, 'head'), may hold values from -0.09375 to 0.09375
- value_weight: bfloat16 [4096, 4096], P(None, 'head'), may hold values from -0.09375 to 0.09375
- write_strength: float32 [32, 16384], P('head', 'seq'), may hold values from 0.0029 to 0.301
- log_decay: float32 [32, 16384], P('head', 'seq'), may hold values from -2 to 0
Outputs:
- mixed_stream: bfloat16 [16384, 4096], P(('seq', 'head'))
- delta_output: bfloat16 [16384, 4096], P('seq', 'head')
The draws below stay inside these ranges and needn't reach their ends.
All inputs are finite; a program needn't handle non-finite values.
Results may differ from the reference program's by a relative error of at most 0.024.
Values may be sent and summed in bfloat16 or wider, within the bound.
No kernel may reach another device: no remote copies, remote signals or barrier semaphores. Data moves between devices by JAX's collectives and lax.ppermute only.
A program may use at most 128 MiB of HBM per device.

```python
import math
import jax
import jax.numpy as jnp
from jax import lax

D = 4096
QUERY_HEADS = 32
KEY_VALUE_HEADS = 8
HK = 8
DELTA_VALUE_HEADS = 32
HEAD_WIDTH = 128
WINDOW_KEYS = 4096
CH = 64
TOK = 512
DOCUMENT_LENGTH = 16384
N_HEAD = 8


def attention_pair(key):
    base = jax.random.fold_in(key, 71)
    query_seed, random_keyset_seed = jax.random.split(base, 2)
    random_keyset = jnp.clip(1.4 * jax.random.normal(random_keyset_seed, (DOCUMENT_LENGTH, KEY_VALUE_HEADS * HEAD_WIDTH), jnp.float32), -6.0, 6.0)
    query_rows_drawn = jnp.clip(1.4 * jax.random.normal(query_seed, (DOCUMENT_LENGTH, QUERY_HEADS * HEAD_WIDTH), jnp.float32), -6.0, 6.0)
    return (query_rows_drawn, random_keyset)


def retaining_heads(key):
    head_seed = jax.random.fold_in(key, 53)
    return jax.random.uniform(head_seed, (DELTA_VALUE_HEADS, 1), jnp.float32) < 0.5


def draw_sliding_query_heads(key, part):
    return attention_pair(key)[0].astype(jnp.bfloat16)


def draw_sliding_key_heads(key, part):
    return attention_pair(key)[1].astype(jnp.bfloat16)


def draw_write_strength(key, part):
    retain = retaining_heads(key)
    key = jax.random.fold_in(key, 43)
    stretch_seeds = jax.random.split(key, 4)
    shape = (DELTA_VALUE_HEADS, DOCUMENT_LENGTH)
    common_rate = jnp.exp(jax.random.uniform(stretch_seeds[0], shape, jnp.float32, math.log(0.02), math.log(0.3)))
    silent_rate = jnp.exp(jax.random.uniform(stretch_seeds[1], shape, jnp.float32, math.log(0.003), math.log(0.01)))
    loud_rate = jnp.exp(jax.random.uniform(stretch_seeds[2], shape, jnp.float32, math.log(0.1), math.log(0.3)))
    starts = jax.random.randint(stretch_seeds[3], (DELTA_VALUE_HEADS, 3), 0, DOCUMENT_LENGTH)
    token_positions = jnp.arange(DOCUMENT_LENGTH)[None, :, None]
    inside = (token_positions >= starts[:, None, :]) & (token_positions < starts[:, None, :] + TOK)
    loud_tokens = jnp.any(inside, axis=-1)
    return jnp.where(retain, jnp.where(loud_tokens, loud_rate, silent_rate), common_rate)


def draw_log_decay(key, part):
    retain = retaining_heads(key)
    random_seeds = jax.random.split(jax.random.fold_in(key, 29), 7)
    share = 0.5
    fast = (jax.random.uniform(random_seeds[0], (DELTA_VALUE_HEADS, 1), jnp.float32) < share) & jnp.logical_not(retain)
    fast_rate = jnp.exp(jax.random.uniform(random_seeds[1], (DELTA_VALUE_HEADS, 1), jnp.float32, math.log(math.log(10.0) / 50.0), math.log(math.log(10.0) / 30.0)))
    slow_rate = jax.random.uniform(random_seeds[2], (DELTA_VALUE_HEADS, 1), jnp.float32, 0.1, 0.2) / DOCUMENT_LENGTH
    arrival_rate = jnp.where(fast, fast_rate, slow_rate)
    split_multiplier = jnp.exp(jax.random.uniform(random_seeds[3], (DELTA_VALUE_HEADS, DOCUMENT_LENGTH // TOK, 1), jnp.float32, 0.0, math.log(2.5)))
    split_multiplier = jnp.broadcast_to(split_multiplier, (DELTA_VALUE_HEADS, DOCUMENT_LENGTH // TOK, TOK)).reshape(DELTA_VALUE_HEADS, DOCUMENT_LENGTH)
    entry_multiplier = jax.random.uniform(random_seeds[4], (DELTA_VALUE_HEADS, DOCUMENT_LENGTH), jnp.float32, 0.5, 1.5)
    cluster_position = jax.random.randint(random_seeds[5], (DELTA_VALUE_HEADS, 2), 0, DOCUMENT_LENGTH)
    cluster_length = jnp.log(1.0 - jax.random.uniform(random_seeds[6], (DELTA_VALUE_HEADS, 2), jnp.float32, 0.2, 0.5))
    token_positions = jnp.arange(DOCUMENT_LENGTH)
    token_clusters = jnp.sum(jnp.where(token_positions[None, :, None] == cluster_position[:, None, :], cluster_length[:, None, :], 0.0), axis=-1)
    return -(arrival_rate * split_multiplier * entry_multiplier) + token_clusters


def block_scale(key, dims, cuts, smallest, largest):
    loudness = 1.0
    for axis_at, blocks in cuts:
        draws = jax.random.uniform(jax.random.fold_in(jax.random.fold_in(key, 6), axis_at), (blocks,), jnp.float32, smallest / len(cuts), largest / len(cuts))
        loudness = loudness * jnp.repeat(jnp.exp(draws), dims[axis_at] // blocks).reshape((-1,) + (1,) * (len(dims) - 1 - axis_at))
    return loudness


def normal_values(rng, extent, deviation, most, pieces=(), kind=jnp.bfloat16):
    entries = deviation * jax.random.normal(rng, extent, jnp.float32)
    if pieces:
        entries = entries * block_scale(rng, extent, pieces, -0.22, 0.18)
    return jnp.clip(entries, -most, most).astype(kind)


def setup_inputs(seed: int = 0) -> dict:
    keys = jax.random.split(jax.random.key(seed), 12)
    return {
        "residual": normal_values(keys[0], (DOCUMENT_LENGTH, D), 1.0, 6.0, ((0, 256),)),
        "sliding_query_heads": draw_sliding_query_heads(jax.random.fold_in(keys[11], 71), 0),
        "sliding_key_heads": draw_sliding_key_heads(jax.random.fold_in(keys[11], 71), 0),
        "sliding_value_heads": normal_values(keys[3], (DOCUMENT_LENGTH, KEY_VALUE_HEADS * HEAD_WIDTH), 1.0, 6.0, ((0, 32), (1, 8))),
        "output_weight": normal_values(keys[4], (QUERY_HEADS * HEAD_WIDTH, D), HEAD_WIDTH ** -0.5, 0.5, ((0, 8),)),
        "norm_gain": jnp.clip(1.0 + 0.1 * jax.random.normal(keys[5], (D,), jnp.float32), 0.5, 1.5),
        "query_weight": normal_values(keys[6], (D, HK * HEAD_WIDTH), D ** -0.5, 0.09375, ((1, 8),)),
        "key_weight": normal_values(keys[7], (D, HK * HEAD_WIDTH), D ** -0.5, 0.09375, ((1, 8),)),
        "value_weight": normal_values(keys[8], (D, DELTA_VALUE_HEADS * HEAD_WIDTH), D ** -0.5, 0.09375, ((1, 8),)),
        "write_strength": draw_write_strength(jax.random.fold_in(keys[11], 71), 0),
        "log_decay": draw_log_decay(jax.random.fold_in(keys[11], 71), 0),
    }


precise = lax.Precision.HIGHEST

def unit_rows(value_rows_drawn):
    return value_rows_drawn / jnp.sqrt(lax.optimization_barrier(jnp.sum(value_rows_drawn * value_rows_drawn, axis=-1, keepdims=True)) + 1e-06)

def stretch_terms(query_rows_drawn, key_rows_drawn, value_rows_drawn, strength, log_decay):
    span_len = query_rows_drawn.shape[1]
    cumul = jnp.cumsum(log_decay, axis=-1)
    later = jnp.arange(span_len)[:, None]
    earlier = jnp.arange(span_len)[None, :]
    strict = (later > earlier)[None]
    within = (later >= earlier)[None]
    spread = cumul[:, :, None] - cumul[:, None, :]
    ratio_within = jnp.where(within, jnp.exp(jnp.where(within, spread, 0.0)), 0.0)
    intersection = jnp.einsum('hcd,hed->hce', key_rows_drawn, key_rows_drawn, precision=precise)
    lower = jnp.where(strict, strength[:, :, None] * ratio_within * intersection, 0.0)
    identity = jnp.eye(span_len, dtype=jnp.float32)[None]
    power = -lower
    inverse = identity + power
    reach = 2
    while reach < span_len:
        power = jnp.einsum('hij,hjk->hik', power, power, precision=precise)
        inverse = jnp.einsum('hij,hjk->hik', inverse, identity + power, precision=precise)
        reach = reach * 2
    transform = inverse * strength[:, None, :]
    growth = jnp.exp(cumul)
    mixed_keys = jnp.einsum('hij,hjd->hid', transform, growth[:, :, None] * key_rows_drawn, precision=precise)
    mixed_values = jnp.einsum('hij,hjd->hid', transform, value_rows_drawn, precision=precise)
    attend = jnp.einsum('hcd,hed->hce', query_rows_drawn, key_rows_drawn, precision=precise) * ratio_within
    reduced = growth[:, :, None] * query_rows_drawn - jnp.einsum('hij,hjd->hid', attend, mixed_keys, precision=precise)
    local_out = jnp.einsum('hij,hjd->hid', attend, mixed_values, precision=precise)
    carried_keys = jnp.exp(cumul[:, -1:] - cumul)[:, :, None] * key_rows_drawn
    final_decay = jnp.exp(cumul[:, -1])
    key_width = key_rows_drawn.shape[2]
    transition = final_decay[:, None, None] * jnp.eye(key_width, dtype=jnp.float32)[None] - jnp.einsum('hcd,hce->hde', carried_keys, mixed_keys, precision=precise)
    injected = jnp.einsum('hcd,hce->hde', carried_keys, mixed_values, precision=precise)
    return (reduced, local_out, transition, injected)

def window_attention(sliding_query_heads, sliding_key_heads, sliding_value_heads):
    block_rows = math.gcd(512, DOCUMENT_LENGTH)
    share_fraction = QUERY_HEADS // KEY_VALUE_HEADS
    query_rows_drawn = sliding_query_heads.reshape(DOCUMENT_LENGTH, KEY_VALUE_HEADS, share_fraction, HEAD_WIDTH)
    filler_length = jnp.zeros((WINDOW_KEYS, KEY_VALUE_HEADS * HEAD_WIDTH), jnp.bfloat16)
    key_rows_drawn = jnp.concatenate([filler_length, sliding_key_heads], axis=0).reshape(-1, KEY_VALUE_HEADS, HEAD_WIDTH)
    value_rows_drawn = jnp.concatenate([filler_length, sliding_value_heads], axis=0).reshape(-1, KEY_VALUE_HEADS, HEAD_WIDTH)

    def one_block(number):
        first = (number * block_rows).astype(jnp.int32)
        query_block = lax.dynamic_slice_in_dim(query_rows_drawn, first, block_rows, 0).astype(jnp.float32)
        key_block = lax.dynamic_slice_in_dim(key_rows_drawn, first, block_rows + WINDOW_KEYS, 0).astype(jnp.float32)
        value_block = lax.dynamic_slice_in_dim(value_rows_drawn, first, block_rows + WINDOW_KEYS, 0).astype(jnp.float32)
        query_pos = first + jnp.arange(block_rows)
        key_pos = first - WINDOW_KEYS + jnp.arange(block_rows + WINDOW_KEYS)
        valid = (key_pos[None, :] <= query_pos[:, None]) & (key_pos[None, :] > query_pos[:, None] - WINDOW_KEYS) & (key_pos[None, :] >= 0)
        scores = jnp.einsum('qgrd,kgd->grqk', query_block, key_block) / math.sqrt(HEAD_WIDTH)
        scores = jnp.where(valid[None, None], scores, -1e+30)
        highest = lax.optimization_barrier(jnp.max(scores, axis=-1, keepdims=True))
        weights = jnp.exp(scores - highest)
        weights = (weights / lax.optimization_barrier(jnp.sum(weights, axis=-1, keepdims=True))).astype(jnp.bfloat16)
        result = jnp.einsum('grqk,kgd->qgrd', weights.astype(jnp.float32), value_block)
        return result.astype(jnp.bfloat16).reshape(block_rows, QUERY_HEADS * HEAD_WIDTH)
    blocks = lax.map(one_block, jnp.arange(DOCUMENT_LENGTH // block_rows, dtype=jnp.int32))
    return blocks.reshape(DOCUMENT_LENGTH, QUERY_HEADS * HEAD_WIDTH)

def reference(residual, sliding_query_heads, sliding_key_heads, sliding_value_heads, output_weight, norm_gain, query_weight, key_weight, value_weight, write_strength, log_decay):
    attended = window_attention(sliding_query_heads, sliding_key_heads, sliding_value_heads)
    group_cols = QUERY_HEADS * HEAD_WIDTH // N_HEAD
    total = jnp.zeros((DOCUMENT_LENGTH, D), jnp.float32)
    for group in range(N_HEAD):
        partial_value = jnp.dot(attended[:, group * group_cols:(group + 1) * group_cols], output_weight[group * group_cols:(group + 1) * group_cols], preferred_element_type=jnp.float32)
        total = total + lax.optimization_barrier(partial_value.astype(jnp.bfloat16)).astype(jnp.float32)
    mixed_stream = (residual.astype(jnp.float32) + total).astype(jnp.bfloat16)
    stream = mixed_stream.astype(jnp.float32)
    normed = (stream * lax.rsqrt(lax.optimization_barrier(jnp.mean(stream * stream, axis=-1, keepdims=True)) + 1e-06) * norm_gain).astype(jnp.bfloat16)
    query_rows_drawn = unit_rows(jnp.dot(normed, query_weight, preferred_element_type=jnp.float32).reshape(DOCUMENT_LENGTH, HK, HEAD_WIDTH))
    key_rows_drawn = unit_rows(jnp.dot(normed, key_weight, preferred_element_type=jnp.float32).reshape(DOCUMENT_LENGTH, HK, HEAD_WIDTH))
    value_rows_drawn = jnp.dot(normed, value_weight, preferred_element_type=jnp.float32).reshape(DOCUMENT_LENGTH, DELTA_VALUE_HEADS, HEAD_WIDTH)
    group_size = DELTA_VALUE_HEADS // HK
    query_rows_drawn = jnp.repeat(query_rows_drawn.transpose(1, 0, 2), group_size, axis=0)
    key_rows_drawn = jnp.repeat(key_rows_drawn.transpose(1, 0, 2), group_size, axis=0)
    value_rows_drawn = value_rows_drawn.transpose(1, 0, 2)
    blocks = DOCUMENT_LENGTH // CH

    def split_blocks(array):
        return array.reshape(DELTA_VALUE_HEADS, blocks, CH, HEAD_WIDTH).transpose(1, 0, 2, 3)
    strength = write_strength.reshape(DELTA_VALUE_HEADS, blocks, CH).transpose(1, 0, 2)
    decays = log_decay.reshape(DELTA_VALUE_HEADS, blocks, CH).transpose(1, 0, 2)

    def advance(state, block):
        reduced, local_out, transition, injected = stretch_terms(*block)
        readout = jnp.einsum('hcd,hde->hce', reduced, state, precision=precise) + local_out
        state = jnp.einsum('hde,hef->hdf', transition, state, precision=precise) + injected
        return (state, readout)
    _, readouts = lax.scan(advance, jnp.zeros((DELTA_VALUE_HEADS, HEAD_WIDTH, HEAD_WIDTH), jnp.float32), (split_blocks(query_rows_drawn), split_blocks(key_rows_drawn), split_blocks(value_rows_drawn), strength, decays))
    delta_output = readouts.transpose(1, 0, 2, 3).reshape(DELTA_VALUE_HEADS, DOCUMENT_LENGTH, HEAD_WIDTH).transpose(1, 0, 2).reshape(DOCUMENT_LENGTH, DELTA_VALUE_HEADS * HEAD_WIDTH)
    return (mixed_stream, delta_output.astype(jnp.bfloat16))
```

```python
import functools
import math

import jax
import jax.numpy as jnp
from jax import lax
from jax.experimental import pallas as pl
from jax.experimental.pallas import tpu as pltpu
from jax.sharding import Mesh
from jax.sharding import PartitionSpec as P

bf = jnp.bfloat16
f32 = jnp.float32
HW = 128
G = 4
WINDOW = 4096
TOK = 512
NEG = -1e30
SCALE = math.log2(math.e) / math.sqrt(HW)
RT = 128
CK = 512
C = 64
W4 = G * C
SEQ = ("x", "y", "c")


def attention_kernel(q0, low_ref, q_ref, own_ref, d2_ref, d4_ref, d6_ref, d8_ref, odd_ref, w_ref, out_ref,
                     keys, values, scores, top, acc, att):
    rows=q_ref.shape[0]
    tiles=rows//RT
    srcs={0:own_ref,2:d2_ref,4:d4_ref,6:d6_ref,8:d8_ref}
    low=low_ref[0]
    lane=lax.broadcasted_iota(jnp.int32,(512,HW),1)
    for d in range(9):
        at=(8-d)*512
        src=srcs[d] if d in srcs else odd_ref.at[(d-1)//2]
        keys[at:at+512,:HW]=src[:,:HW]
        values[at:at+512,:HW]=src[:,HW:]
        gone=jnp.where(at<low,NEG,0.0)
        keys[at:at+512,HW:]=jnp.where(lane==0,gone,0.0).astype(jnp.bfloat16)
        values[at:at+512,HW:]=jnp.ones((512,HW),jnp.bfloat16)
    r=lax.broadcasted_iota(jnp.int32,(G*RT,HW),0)%RT
    c=lax.broadcasted_iota(jnp.int32,(G*RT,HW),1)
    oldest=c>r
    unit=jnp.where(c==0,1.0,0.0).astype(jnp.bfloat16)

    def queries(t):
        q=q_ref[t*RT:(t+1)*RT,:]
        q=jnp.concatenate([q[:,h*HW:(h+1)*HW] for h in range(G)],axis=0)
        return jnp.concatenate([q,unit],axis=1)

    def dot_t(a,b):
        return lax.dot_general(a,b,(((1,),(1,)),((),())),preferred_element_type=jnp.float32)

    def score(t,j,first):
        base=q0+t*RT
        at=base+j*CK if isinstance(j,int) else pl.multiple_of(base+j*CK,RT)
        s=dot_t(queries(t),keys[pl.ds(at,CK),:])
        if first:
            last=dot_t(queries(t),keys[pl.ds(base+4096,RT),:])
            s=jnp.concatenate([jnp.where(oldest,s[:,:HW],last),s[:,HW:]],axis=1)
        scores[t%2,:,pl.ds(j*CK if isinstance(j,int) else pl.multiple_of(j*CK,CK),CK)]=s
        m=functools.reduce(jnp.maximum,[s[:,i*HW:(i+1)*HW] for i in range(CK//HW)])
        if first: top[t%2]=m
        else: top[t%2]=jnp.maximum(top[t%2],m)

    def weigh(t,j,first,m):
        base=q0+t*RT
        at=base+j*CK if isinstance(j,int) else pl.multiple_of(base+j*CK,RT)
        s=scores[t%2,:,pl.ds(j*CK if isinstance(j,int) else pl.multiple_of(j*CK,CK),CK)]
        p=jnp.concatenate([jnp.exp2((s[:,i*HW:(i+1)*HW]-m)*SCALE) for i in range(CK//HW)],axis=1).astype(jnp.bfloat16)
        if first:
            pa=p[:,:HW]
            zero=jnp.zeros_like(pa)
            new=jnp.where(oldest,zero,pa)
            old=jnp.where(oldest,pa,zero)
            p=jnp.concatenate([old,p[:,HW:],new],axis=1)
            v=jnp.concatenate([values[pl.ds(at,CK),:],values[pl.ds(base+4096,RT),:]],axis=0)
            acc[...]=jnp.dot(p,v,preferred_element_type=jnp.float32)
        else:
            acc[...]+=jnp.dot(p,values[pl.ds(at,CK),:],preferred_element_type=jnp.float32)


    steps=4096//CK
    score(0,0,True)
    def pre(j,_):
        score(0,j,False)
        return _
    lax.fori_loop(1,steps,pre,0)
    for t in range(tiles):
        m=jnp.broadcast_to(jnp.max(top[t%2],axis=1,keepdims=True),(G*RT,HW))
        top[t%2]=m
        weigh(t,0,True,m)
        if t+1<tiles: score(t+1,0,True)
        def step(j,_):
            weigh(t,j,False,top[t%2])
            if t+1<tiles: score(t+1,j,False)
            return _
        lax.fori_loop(1,steps,step,0)
        a=acc[...]
        o=(a[:,:HW]/a[:,HW:]).astype(jnp.bfloat16)
        for h in range(G):
            att[t*RT:(t+1)*RT,h*HW:(h+1)*HW]=o[h*RT:(h+1)*RT]
    out_ref[...]=jnp.dot(att[...],w_ref[...],preferred_element_type=jnp.float32).astype(jnp.bfloat16)

def attention(q0,low,q,own,d2,d4,d6,d8,odd,w):
    rows=q.shape[0]
    vm=pl.BlockSpec(memory_space=pltpu.VMEM)
    return pl.pallas_call(
        functools.partial(attention_kernel,q0),
        out_shape=jax.ShapeDtypeStruct((rows,w.shape[1]),jnp.bfloat16),
        in_specs=[pl.BlockSpec(memory_space=pltpu.SMEM)]+[vm]*8,
        out_specs=vm,
        scratch_shapes=[
            pltpu.VMEM((9*512,2*HW),jnp.bfloat16),
            pltpu.VMEM((9*512,2*HW),jnp.bfloat16),
            pltpu.VMEM((2,G*RT,4096),jnp.float32),
            pltpu.VMEM((2,G*RT,HW),jnp.float32),
            pltpu.VMEM((G*RT,2*HW),jnp.float32),
            pltpu.VMEM((rows,G*HW),jnp.bfloat16),
        ],
        compiler_params=pltpu.CompilerParams(vmem_limit_bytes=60<<20),
    )(low,q,own,d2,d4,d6,d8,odd,w)


def mm(a,b):
    return jnp.dot(a.astype(bf),b.astype(bf),preferred_element_type=f32)
def mm_t(a,b):
    return lax.dot_general(a.astype(bf),b.astype(bf),(((1,),(1,)),((),())),preferred_element_type=f32)
def tmm(a,b):
    return lax.dot_general(a.astype(bf),b.astype(bf),(((0,),(0,)),((),())),preferred_element_type=f32)

def delta_kernel(lift_ref, cumr_ref, cumc_ref, lastc_ref, strc_ref, maps_ref, twist_ref, local_ref, mixed_s, red_s, loc_s, tx_s):
    blocks=lift_ref.shape[0]//C
    i=lax.broadcasted_iota(jnp.int32,(W4,W4),0)
    j=lax.broadcasted_iota(jnp.int32,(W4,W4),1)
    within=(i>=j)&(i//C==j//C)
    strict=(i>j)&(i//C==j//C)
    levels=[]
    size=1
    while size<C:
        levels.append((i//(2*size)==j//(2*size))&(i//size!=j//size)&(i>j))
        size*=2
    eye=jnp.where(i==j,1.0,0.0).astype(f32)
    def unit(x):
        return x/jnp.sqrt(jnp.sum(x*x,axis=1,keepdims=True)+1e-6)
    K=[];Q=[];R=[];L=[];A=[]
    for n in range(blocks):
        rows=slice(n*C,(n+1)*C)
        q=unit(lift_ref[rows,:HW]); k=unit(lift_ref[rows,HW:2*HW])
        k4=jnp.concatenate([k]*G,axis=0); q4=jnp.concatenate([q]*G,axis=0)
        v4=jnp.concatenate([lift_ref[rows,(2+h)*HW:(3+h)*HW] for h in range(G)],axis=0)
        cc=cumc_ref[:,n:n+1]; cr=cumr_ref[n:n+1,:]; b=strc_ref[:,n:n+1]
        ratio=jnp.where(within,jnp.exp(jnp.where(within,cc-cr,0.0)),0.0)
        L.append(jnp.where(strict,b*ratio*mm_t(k4,k4),0.0))
        A.append((mm_t(q4,k4)*ratio).astype(bf))
        growth=jnp.exp(cc)
        R.append(jnp.concatenate([(b*growth)*k4,b*v4],axis=1).astype(bf))
        Q.append(growth*q4)
        K.append((jnp.exp(lastc_ref[:,n:n+1]-cc)*k4).astype(bf))
    X=[eye-jnp.where(levels[0],L[n],0.0) for n in range(blocks)]
    for mask in levels[1:]:
        Y=[mm(X[n],jnp.where(mask,L[n],0.0)) for n in range(blocks)]
        X=[X[n]-mm(Y[n],X[n]) for n in range(blocks)]
    M=[mm(X[n],R[n]) for n in range(blocks)]
    S=[mm(A[n],M[n]) for n in range(blocks)]
    state=[None]*G
    ii=lax.broadcasted_iota(jnp.int32,(HW,2*HW),0)
    jj=lax.broadcasted_iota(jnp.int32,(HW,2*HW),1)
    start=jnp.where(ii==jj,1.0,0.0).astype(f32)
    state=[start]*G
    right=jj>=HW
    for n in range(blocks):
        red=Q[n]-S[n][:,:HW]
        for h in range(G):
            hr=slice(h*C,(h+1)*C)
            t=tmm(K[n][hr],M[n][hr])
            last=jnp.exp(lastc_ref[h*C:h*C+1,n:n+1])
            both=mm(jnp.concatenate([red[hr],t[:,:HW]],axis=0),state[h])
            twist_ref[h,n*C:(n+1)*C,:]=both[:C,:HW].astype(bf)
            local_ref[n*C:(n+1)*C,h*HW:(h+1)*HW]=both[:C,HW:]+S[n][hr,HW:]
            state[h]=last*state[h]-both[C:]+jnp.where(right,t,0.0)
    for h in range(G):
        maps_ref[h]=state[h].astype(bf)

def delta_local(lift,cumr,cumc,lastc,strc):
    rows=lift.shape[0]
    vm=pl.BlockSpec(memory_space=pltpu.VMEM)
    return pl.pallas_call(
        delta_kernel,
        out_shape=(jax.ShapeDtypeStruct((G,HW,2*HW),bf),jax.ShapeDtypeStruct((G,rows,HW),bf),jax.ShapeDtypeStruct((rows,G*HW),f32)),
        in_specs=[vm]*5,out_specs=(vm,vm,vm),
        scratch_shapes=[pltpu.VMEM((8,128),f32)]*4,
        compiler_params=pltpu.CompilerParams(vmem_limit_bytes=60<<20),
    )(lift,cumr,cumc,lastc,strc)

def decay_terms(write_strength,log_decay,C=64):
    g,rows=log_decay.shape
    blocks=rows//C
    cum=jnp.cumsum(log_decay.reshape(g,blocks,C),axis=-1)
    last=jnp.broadcast_to(cum[:,:,-1:],cum.shape)
    col=lambda a: a.transpose(0,2,1).reshape(g*C,blocks)
    return (cum.transpose(1,0,2).reshape(blocks,g*C),col(cum),col(last),col(write_strength.reshape(g,blocks,C)))


def spread(before, later):
    high = before.astype(bf)
    low = (before - high.astype(f32)).astype(bf)
    m = later[:, :HW]
    return (jnp.dot(m, high, preferred_element_type=f32)
            + jnp.dot(m, low, preferred_element_type=f32))


def with_injected(before, later):
    n = later[:, HW:].astype(f32)
    return spread(before, later) + jnp.concatenate([jnp.zeros_like(n), n], axis=1)


def chip_kernel(at_ref, own_ref, other_ref, first_ref, total_ref):
    c = at_ref[2]
    for h in range(2):
        own, other = own_ref[2 * c + h], other_ref[h]
        first = jnp.where(c == 0, own, other)
        second = jnp.where(c == 0, other, own)
        first_ref[h] = first
        total_ref[h] = with_injected(first.astype(f32), second).astype(bf)


def row_kernel(at_ref, t0_ref, t1_ref, t2_ref, t3_ref, prefix_ref, total_ref, parts):
    y = at_ref[1]
    for r, t in enumerate((t0_ref, t1_ref, t2_ref, t3_ref)):
        parts[lax.rem(y - r + 4, 4)] = t[...]
    i = lax.broadcasted_iota(jnp.int32, (HW, 2 * HW), 0)
    j = lax.broadcasted_iota(jnp.int32, (HW, 2 * HW), 1)
    start = jnp.where(i == j, 1.0, 0.0).astype(f32)
    for h in range(2):
        now = start
        kept = start
        for k in range(4):
            kept = jnp.where(k == y, now, kept)
            now = with_injected(now, parts[k, h])
        prefix_ref[h] = kept
        total_ref[h] = now.astype(bf)


def column_kernel(at_ref, x1_ref, x2_ref, x3_ref, prefix_ref, first_ref, mine_ref, other_ref):
    x, c = at_ref[0], at_ref[2]
    for h in range(2):
        state = jnp.zeros((HW, HW), f32)
        for d, t in ((3, x3_ref), (2, x2_ref), (1, x1_ref)):
            new = spread(state, t[h]) + t[h, :, HW:].astype(f32)
            state = jnp.where(x >= d, new, state)
        p = prefix_ref[h]
        p_high = p[:, :HW].astype(bf)
        p_low = (p[:, :HW] - p_high.astype(f32)).astype(bf)
        s = state.astype(bf)
        s_low = (state - s.astype(f32)).astype(bf)
        zero = (jnp.dot(p_high, s, preferred_element_type=f32)
                + jnp.dot(p_low, s, preferred_element_type=f32)
                + jnp.dot(p_high, s_low, preferred_element_type=f32) + p[:, HW:])
        one = spread(zero, first_ref[h]) + first_ref[h, :, HW:].astype(f32)
        mine_ref[h] = jnp.where(c == 0, zero, one).astype(bf)
        other_ref[h] = jnp.where(c == 0, one, zero).astype(bf)


def readout_kernel(at_ref, mine_ref, other_ref, twist_ref, local_ref, out_ref):
    c = at_ref[2]
    for h in range(G):
        own = (h // 2) == c
        state = jnp.where(own, mine_ref[h % 2], other_ref[h % 2])
        cols = slice(h * HW, (h + 1) * HW)
        out_ref[:, cols] = (local_ref[:, cols] + jnp.dot(
            twist_ref[h], state, preferred_element_type=f32)).astype(bf)


def norm_kernel(residual_ref, sum_ref, gain_ref, mixed_ref, normed_ref):
    mixed = (residual_ref[...].astype(f32) + sum_ref[...].astype(f32)).astype(bf)
    mixed_ref[...] = mixed
    stream = mixed.astype(f32)
    scale = lax.rsqrt(jnp.mean(stream * stream, axis=-1, keepdims=True) + 1e-06)
    normed_ref[...] = (stream * scale * gain_ref[...]).astype(bf)


VM = pl.BlockSpec(memory_space=pltpu.VMEM)
SM = pl.BlockSpec(memory_space=pltpu.SMEM)


def local_call(kernel, shapes, scalars, *arrays, scratch=()):
    return pl.pallas_call(
        kernel,
        out_shape=shapes,
        in_specs=[SM] * len(scalars) + [VM] * len(arrays),
        out_specs=jax.tree.map(lambda _: VM, shapes),
        scratch_shapes=list(scratch),
        compiler_params=pltpu.CompilerParams(vmem_limit_bytes=48 << 20),
    )(*scalars, *arrays)


def shape(dims, kind=bf):
    return jax.ShapeDtypeStruct(dims, kind)


def rotated(array, axis, by):
    n = lax.axis_size(axis)
    return lax.ppermute(array, axis, [(i, (i + by) % n) for i in range(n)])


def shifted(array, axis, by):
    n = lax.axis_size(axis)
    return lax.ppermute(array, axis, [(i, i + by) for i in range(n - by)])


def earlier_rows(own):
    y, c = lax.axis_index("y"), lax.axis_index("c")
    count = lax.axis_size("y")
    above = shifted(own, "x", 1)
    d = {8: above}
    for r in (1, 2, 3):
        d[2 * r] = rotated(jnp.where(y + r >= count, above, own), "y", r)
    odd = jnp.where(
        c == 0,
        jnp.stack([own, d[2], d[4], d[6]]),
        jnp.stack([d[2], d[4], d[6], d[8]]),
    )
    return d, rotated(odd, "c", 1)


def incoming_state(at, maps):
    c = at[2]
    theirs = rotated(lax.dynamic_slice_in_dim(maps, 2 * (1 - c), 2, 0), "c", 1)
    two = shape((2, HW, 2 * HW))
    first, total = local_call(chip_kernel, (two, two), (at,), maps, theirs)
    parts = [total] + [rotated(total, "y", r) for r in (1, 2, 3)]
    prefix, row = local_call(
        row_kernel, (shape((2, HW, 2 * HW), f32), two), (at,), *parts,
        scratch=[pltpu.VMEM((4, 2, HW, 2 * HW), bf)],
    )
    rows = [shifted(row, "x", d) for d in (1, 2, 3)]
    square = shape((2, HW, HW))
    mine, other = local_call(column_kernel, (square, square), (at,), *rows, prefix, first)
    return mine, rotated(other, "c", 1)


def body(
    residual,
    sliding_query_heads,
    sliding_key_heads,
    sliding_value_heads,
    output_weight,
    norm_gain,
    query_weight,
    key_weight,
    value_weight,
    write_strength,
    log_decay,
):
    x, y, c = (lax.axis_index(a) for a in SEQ)
    at = jnp.stack([x, y, c]).astype(jnp.int32)
    shard = (x * lax.axis_size("y") + y) * 2 + c
    low = jnp.maximum(0, (WINDOW // TOK - shard) * TOK).astype(jnp.int32)[None]
    own = jnp.concatenate([sliding_key_heads, sliding_value_heads], axis=1)
    d, odd = earlier_rows(own)
    weights = jnp.concatenate([query_weight, key_weight, value_weight], axis=1)
    terms = decay_terms(write_strength, log_decay)
    projected = attention(
        0, low, sliding_query_heads, own, d[2], d[4], d[6], d[8], odd, output_weight)
    summed = lax.psum_scatter(projected, "head", scatter_dimension=0, tiled=True)
    mixed_stream, normed = local_call(
        norm_kernel, (shape(residual.shape), shape(residual.shape)), (),
        residual, summed, norm_gain[None, :])
    piece = lax.all_gather(normed, "head", axis=0, tiled=True)
    lifted = jnp.dot(piece, weights, preferred_element_type=f32)
    maps, twisted, local = delta_local(lifted, *terms)
    mine, other = incoming_state(at, maps)
    delta_output = local_call(
        readout_kernel, shape((lifted.shape[0], G * HW)), (at,), mine, other, twisted, local)
    return mixed_stream, delta_output


def solution(mesh):
    devices = mesh.devices.reshape(4, 4, 2, 8)
    split = Mesh(devices, SEQ + ("head",))
    in_specs = (
        P(SEQ + ("head",), None),
        P(SEQ, "head"),
        P(SEQ, "head"),
        P(SEQ, "head"),
        P("head", None),
        P(),
        P(None, "head"),
        P(None, "head"),
        P(None, "head"),
        P("head", SEQ),
        P("head", SEQ),
    )
    out_specs = (P(SEQ + ("head",), None), P(SEQ, "head"))
    return jax.shard_map(body, mesh=split, in_specs=in_specs, out_specs=out_specs, check_vma=False)
```

```python
import functools
import math

import jax
import jax.numpy as jnp
from jax import lax
from jax.experimental import pallas as pl
from jax.experimental.pallas import tpu as pltpu
from jax.sharding import Mesh
from jax.sharding import PartitionSpec as P

bf = jnp.bfloat16
f32 = jnp.float32
HW = 128
G = 4
WINDOW = 4096
TOK = 512
NEG = -1e30
SCALE = math.log2(math.e) / math.sqrt(HW)
RT = 64
HALF = 2048
KSTEPS = 4
KROWS = 2 * HALF // KSTEPS
CK = 4096
C = 64
W4 = G * C
SEQ = ("x", "y", "c")


def window_kernel(low_ref, own_ref, d2_ref, d4_ref, d6_ref, d8_ref, odd_ref, keys, values, sems):
    even = {0: own_ref, 2: d2_ref, 4: d4_ref, 6: d6_ref, 8: d8_ref}
    lane = lax.broadcasted_iota(jnp.int32, (TOK, HW), 1)
    copies = []
    for d in range(9):
        rows = pl.ds((8 - d) * TOK, TOK)
        src = even[d] if d in even else odd_ref.at[(d - 1) // 2]
        for n, dst in enumerate((keys, values)):
            copies.append(pltpu.make_async_copy(
                src.at[:, pl.ds(n * HW, HW)], dst.at[rows, pl.ds(0, HW)], sems.at[d, n]))
    for copy in copies:
        copy.start()
    for d in range(9):
        rows = slice((8 - d) * TOK, (9 - d) * TOK)
        bias = jnp.where((8 - d) * TOK < low_ref[0], NEG, 0.0)
        keys[rows, HW:] = jnp.where(lane == 0, bias, 0.0).astype(bf)
        values[rows, HW:] = jnp.ones((TOK, HW), bf)
    for copy in copies:
        copy.wait()


def attention_kernel(count, blocks_ref, q_ref, keys, values, w_ref, *rest):
    outs, (scores, top, acc, att) = rest[: 2 * count], rest[2 * count :]
    r = lax.broadcasted_iota(jnp.int32, (G * RT, HW), 0) % RT
    c = lax.broadcasted_iota(jnp.int32, (G * RT, HW), 1)
    unit = jnp.where(c == 0, 1.0, 0.0).astype(bf)
    steps = WINDOW // CK

    def place(t):
        block = blocks_ref[t]
        half = lax.rem(block, 2)
        return pl.multiple_of((block - half) * RT, 2 * RT), c > r + half * RT

    def queries(t):
        q = q_ref[pl.ds(pl.multiple_of(blocks_ref[t] * RT, RT), RT), :]
        q = jnp.concatenate([q[:, h * HW : (h + 1) * HW] for h in range(G)], axis=0)
        return jnp.concatenate([q, unit], axis=1)

    def dot_t(a, b):
        return lax.dot_general(a, b, (((1,), (1,)), ((), ())), preferred_element_type=f32)

    def columns(j):
        return pl.ds(j * CK if isinstance(j, int) else pl.multiple_of(j * CK, CK), CK)

    def score(t, j):
        base, oldest = place(t)
        q = queries(t)
        s = dot_t(q, keys[pl.ds(pl.multiple_of(base + j * CK, 2 * RT), CK), :])
        first = isinstance(j, int)
        if first:
            newest = dot_t(q, keys[pl.ds(pl.multiple_of(base + WINDOW, 2 * RT), HW), :])
            s = jnp.concatenate([jnp.where(oldest, s[:, :HW], newest), s[:, HW:]], axis=1)
        scores[t % 2, :, columns(j)] = s
        m = functools.reduce(
            jnp.maximum, [s[:, i * HW : (i + 1) * HW] for i in range(CK // HW)])
        top[t % 2] = m if first else jnp.maximum(top[t % 2], m)

    def weigh(t, j, m):
        base, oldest = place(t)
        v = values[pl.ds(pl.multiple_of(base + j * CK, 2 * RT), CK), :]
        s = scores[t % 2, :, columns(j)]
        p = jnp.concatenate(
            [jnp.exp2((s[:, i * HW : (i + 1) * HW] - m) * SCALE) for i in range(CK // HW)], axis=1)
        if isinstance(j, int):
            edge = p[:, :HW]
            old = jnp.where(oldest, edge, 0.0)
            p = jnp.concatenate([old, p[:, HW:], edge - old], axis=1)
            v = jnp.concatenate(
                [v, values[pl.ds(pl.multiple_of(base + WINDOW, 2 * RT), HW), :]], axis=0)
            acc[...] = jnp.dot(p.astype(bf), v, preferred_element_type=f32)
        else:
            acc[...] += jnp.dot(p.astype(bf), v, preferred_element_type=f32)

    def pre(j, _):
        score(0, j)
        return _

    score(0, 0)
    lax.fori_loop(1, steps, pre, 0)
    for t in range(count):
        m = jnp.broadcast_to(jnp.max(top[t % 2], axis=1, keepdims=True), (G * RT, HW))
        top[t % 2] = m
        weigh(t, 0, m)
        if t + 1 < count:
            score(t + 1, 0)

        def step(j, _):
            weigh(t, j, top[t % 2])
            if t + 1 < count:
                score(t + 1, j)
            return _

        lax.fori_loop(1, steps, step, 0)
        a = acc[...]
        o = (a[:, :HW] / a[:, HW:]).astype(bf)
        for h in range(G):
            att[t * RT : (t + 1) * RT, h * HW : (h + 1) * HW] = o[h * RT : (h + 1) * RT]
    for n in range(2):
        part = jnp.dot(
            att[...], w_ref[:, n * HALF : (n + 1) * HALF], preferred_element_type=f32).astype(bf)
        for t in range(count):
            outs[2 * t + n][...] = part[t * RT : (t + 1) * RT]


def mm(a, b):
    return jnp.dot(a.astype(bf), b.astype(bf), preferred_element_type=f32)


def mm_t(a, b):
    return lax.dot_general(
        a.astype(bf), b.astype(bf), (((1,), (1,)), ((), ())), preferred_element_type=f32)


def tmm(a, b):
    return lax.dot_general(
        a.astype(bf), b.astype(bf), (((0,), (0,)), ((), ())), preferred_element_type=f32)


def unit_rows(rows):
    return rows / jnp.sqrt(jnp.sum(rows * rows, axis=1, keepdims=True) + 1e-6)


def block_kernel(count, blocks_ref, *refs):
    pieces = refs[: 2 * count]
    row_ref, col_ref, *far, reduced_ref, local_ref, map_ref, w, sems = refs[2 * count :]
    copies = []
    for n in range(KSTEPS):
        rows = pl.ds(n * KROWS, KROWS)
        at = 0
        for m, ref in enumerate(far):
            width = ref.shape[1]
            copies.append(pltpu.make_async_copy(
                ref.at[rows, :], w.at[rows, pl.ds(at, width)], sems.at[n, m]))
            at += width
    for copy in copies:
        copy.start()
    a = jnp.concatenate([pieces[2 * t][...] for t in range(count)], axis=0)
    b = jnp.concatenate([pieces[2 * t + 1][...] for t in range(count)], axis=0)
    row = jnp.concatenate([a, b], axis=1)
    lifted = 0.0
    for n in range(KSTEPS):
        for copy in copies[len(far) * n : len(far) * (n + 1)]:
            copy.wait()
        cols = slice(n * KROWS, (n + 1) * KROWS)
        lifted += jnp.dot(row[:, cols], w[cols, :], preferred_element_type=f32)
    i = lax.broadcasted_iota(jnp.int32, (W4, W4), 0)
    j = lax.broadcasted_iota(jnp.int32, (W4, W4), 1)
    within = (i >= j) & (i // C == j // C)
    levels = []
    size = 1
    while size < C:
        levels.append((i // (2 * size) == j // (2 * size)) & (i // size != j // size) & (i > j))
        size *= 2
    eye = jnp.where(i == j, 1.0, 0.0).astype(f32)
    sides, scaled, carried, lower, attend = [], [], [], [], []
    for t in range(count):
        rows = lifted[t * C : (t + 1) * C]
        q4 = jnp.concatenate([unit_rows(rows[:, :HW])] * G, axis=0)
        k4 = jnp.concatenate([unit_rows(rows[:, HW : 2 * HW])] * G, axis=0)
        v4 = jnp.concatenate([rows[:, (2 + h) * HW : (3 + h) * HW] for h in range(G)], axis=0)
        col = col_ref[blocks_ref[t]]
        cum, last, strength = col[:, :1], col[:, 1:2], col[:, 2:3]
        ratio = jnp.where(
            within, jnp.exp(jnp.where(within, cum - row_ref[blocks_ref[t]], 0.0)), 0.0)
        lower.append(strength * ratio * mm_t(k4, k4))
        attend.append((mm_t(q4, k4) * ratio).astype(bf))
        growth = jnp.exp(cum)
        sides.append(
            jnp.concatenate([(strength * growth) * k4, strength * v4], axis=1).astype(bf))
        scaled.append(growth * q4)
        carried.append((jnp.exp(last - cum) * k4).astype(bf))
    inverse = [eye - jnp.where(levels[0], low, 0.0) for low in lower]
    for mask in levels[1:]:
        moved = [mm(x, jnp.where(mask, low, 0.0)) for x, low in zip(inverse, lower)]
        inverse = [x - mm(y, x) for x, y in zip(inverse, moved)]
    mixed = [mm(x, side).astype(bf) for x, side in zip(inverse, sides)]
    seen = [mm(near, mix) for near, mix in zip(attend, mixed)]
    for t in range(count):
        reduced_ref[t] = (scaled[t] - seen[t][:, :HW]).astype(bf)
        local_ref[t] = seen[t][:, HW:]
        for h in range(G):
            rows = slice(h * C, (h + 1) * C)
            map_ref[t, h] = tmm(carried[t][rows], mixed[t][rows]).astype(bf)


def chain_kernel(offsets, at_ref, col_ref, *refs):
    n = sum(offsets, ())
    parts, refs = refs[: 3 * len(offsets)], refs[3 * len(offsets) :]
    maps_ref, twist_ref, out_ref, reduced, local, maps = refs
    blocks = len(n)
    for k, group in enumerate(offsets):
        for t, offset in enumerate(group):
            at = lax.rem(at_ref[3] + offset + blocks, blocks)
            reduced[at] = parts[3 * k][t]
            local[at] = parts[3 * k + 1][t]
            maps[at] = parts[3 * k + 2][t]
    i = lax.broadcasted_iota(jnp.int32, (HW, 2 * HW), 0)
    j = lax.broadcasted_iota(jnp.int32, (HW, 2 * HW), 1)
    state = [jnp.where(i == j, 1.0, 0.0).astype(f32)] * G
    for n in range(blocks):
        for h in range(G):
            rows = slice(h * C, (h + 1) * C)
            m = maps[n, h]
            decay = jnp.exp(col_ref[n, h * C : h * C + 1, 1:2])
            both = mm(jnp.concatenate([reduced[n, rows], m[:, :HW]], axis=0), state[h])
            twist_ref[h, n * C : (n + 1) * C, :] = both[:C, :HW].astype(bf)
            out_ref[n * C : (n + 1) * C, h * HW : (h + 1) * HW] = both[:C, HW:] + local[n, rows]
            state[h] = decay * state[h] - both[C:] + jnp.where(j >= HW, m.astype(f32), 0.0)
    for h in range(G):
        maps_ref[h] = state[h].astype(bf)


def decay_terms(write_strength, log_decay):
    g, rows = log_decay.shape
    blocks = rows // C
    cum = jnp.cumsum(log_decay.reshape(g, blocks, C), axis=-1)
    last = jnp.broadcast_to(cum[:, :, -1:], cum.shape)
    strength = write_strength.reshape(g, blocks, C)
    col = jnp.stack([cum, last, strength], axis=-1).transpose(1, 0, 2, 3)
    return cum.transpose(1, 0, 2).reshape(blocks, 1, g * C), col.reshape(blocks, g * C, 3)


def spread(before, later):
    high = before.astype(bf)
    low = (before - high.astype(f32)).astype(bf)
    m = later[:, :HW]
    return (jnp.dot(m, high, preferred_element_type=f32)
            + jnp.dot(m, low, preferred_element_type=f32))


def with_injected(before, later):
    n = later[:, HW:].astype(f32)
    return spread(before, later) + jnp.concatenate([jnp.zeros_like(n), n], axis=1)


def chip_kernel(at_ref, own_ref, other_ref, first_ref, total_ref):
    c = at_ref[2]
    for h in range(2):
        own, other = own_ref[2 * c + h], other_ref[h]
        first = jnp.where(c == 0, own, other)
        second = jnp.where(c == 0, other, own)
        first_ref[h] = first
        total_ref[h] = with_injected(first.astype(f32), second).astype(bf)


def row_kernel(at_ref, t0_ref, t1_ref, t2_ref, t3_ref, prefix_ref, total_ref, parts):
    y = at_ref[1]
    for r, t in enumerate((t0_ref, t1_ref, t2_ref, t3_ref)):
        parts[lax.rem(y - r + 4, 4)] = t[...]
    i = lax.broadcasted_iota(jnp.int32, (HW, 2 * HW), 0)
    j = lax.broadcasted_iota(jnp.int32, (HW, 2 * HW), 1)
    start = jnp.where(i == j, 1.0, 0.0).astype(f32)
    for h in range(2):
        now = start
        kept = start
        for k in range(4):
            kept = jnp.where(k == y, now, kept)
            now = with_injected(now, parts[k, h])
        prefix_ref[h] = kept
        total_ref[h] = now.astype(bf)


def column_kernel(at_ref, x1_ref, x2_ref, x3_ref, prefix_ref, first_ref, mine_ref, other_ref):
    x, c = at_ref[0], at_ref[2]
    for h in range(2):
        state = jnp.zeros((HW, HW), f32)
        for d, t in ((3, x3_ref), (2, x2_ref), (1, x1_ref)):
            new = spread(state, t[h]) + t[h, :, HW:].astype(f32)
            state = jnp.where(x >= d, new, state)
        p = prefix_ref[h]
        p_high = p[:, :HW].astype(bf)
        p_low = (p[:, :HW] - p_high.astype(f32)).astype(bf)
        s = state.astype(bf)
        s_low = (state - s.astype(f32)).astype(bf)
        zero = (jnp.dot(p_high, s, preferred_element_type=f32)
                + jnp.dot(p_low, s, preferred_element_type=f32)
                + jnp.dot(p_high, s_low, preferred_element_type=f32) + p[:, HW:])
        one = spread(zero, first_ref[h]) + first_ref[h, :, HW:].astype(f32)
        mine_ref[h] = jnp.where(c == 0, zero, one).astype(bf)
        other_ref[h] = jnp.where(c == 0, one, zero).astype(bf)


def readout_kernel(at_ref, mine_ref, other_ref, twist_ref, local_ref, out_ref):
    c = at_ref[2]
    for h in range(G):
        own = (h // 2) == c
        state = jnp.where(own, mine_ref[h % 2], other_ref[h % 2])
        cols = slice(h * HW, (h + 1) * HW)
        out_ref[:, cols] = (local_ref[:, cols] + jnp.dot(
            twist_ref[h], state, preferred_element_type=f32)).astype(bf)


def norm_kernel(*refs):
    *sums, residual_ref, gain_ref, mixed_ref, a_ref, b_ref = refs
    total = residual_ref[...].astype(f32) + jnp.concatenate(
        [sum(s[...].astype(f32) for s in sums[n::2]) for n in range(2)], axis=1)
    mixed = total.astype(bf)
    mixed_ref[...] = mixed
    stream = mixed.astype(f32)
    scale = lax.rsqrt(jnp.mean(stream * stream, axis=-1, keepdims=True) + 1e-06)
    normed = (stream * scale * gain_ref[...]).astype(bf)
    a_ref[...] = normed[:, :HALF]
    b_ref[...] = normed[:, HALF:]


VM = pl.BlockSpec(memory_space=pltpu.VMEM)
SM = pl.BlockSpec(memory_space=pltpu.SMEM)


def local_call(kernel, shapes, scalars, *arrays, scratch=(), flops=0, after=(), far=(), mib=12):
    if after:
        held = kernel
        spot = len(scalars) + len(arrays) + len(far)

        def kernel(*refs):
            held(*refs[:spot], *refs[spot + len(after) :])

    cost = pl.CostEstimate(flops=flops, bytes_accessed=1 << 20, transcendentals=0)
    return pl.pallas_call(
        kernel,
        cost_estimate=cost if flops else None,
        out_shape=shapes,
        in_specs=[SM] * len(scalars) + [VM] * len(arrays) + [pl.BlockSpec(memory_space=pl.ANY)] * (len(far) + len(after)),
        out_specs=jax.tree.map(lambda _: VM, shapes),
        scratch_shapes=list(scratch),
        compiler_params=pltpu.CompilerParams(vmem_limit_bytes=mib << 20),
    )(*scalars, *arrays, *far, *after)


def shape(dims, kind=bf):
    return jax.ShapeDtypeStruct(dims, kind)


def rotated(array, axis, by):
    n = lax.axis_size(axis)
    return lax.ppermute(array, axis, [(i, (i + by) % n) for i in range(n)])


def shifted(array, axis, by):
    n = lax.axis_size(axis)
    return lax.ppermute(array, axis, [(i, i + by) for i in range(n - by)])


def earlier_rows(own):
    y, c = lax.axis_index("y"), lax.axis_index("c")
    count = lax.axis_size("y")
    above = shifted(own, "x", 1)
    d = {8: above}
    for r in (1, 2, 3):
        d[2 * r] = rotated(jnp.where(y + r >= count, above, own), "y", r)
    odd = jnp.where(
        c == 0,
        jnp.stack([own, d[2], d[4], d[6]]),
        jnp.stack([d[2], d[4], d[6], d[8]]),
    )
    return d, rotated(odd, "c", 1)


def incoming_state(at, maps):
    c = at[2]
    theirs = rotated(lax.dynamic_slice_in_dim(maps, 2 * (1 - c), 2, 0), "c", 1)
    two = shape((2, HW, 2 * HW))
    first, total = local_call(chip_kernel, (two, two), (at,), maps, theirs)
    parts = [total] + [rotated(total, "y", r) for r in (1, 2, 3)]
    prefix, row = local_call(
        row_kernel, (shape((2, HW, 2 * HW), f32), two), (at,), *parts,
        scratch=[pltpu.VMEM((4, 2, HW, 2 * HW), bf)],
    )
    rows = [shifted(row, "x", d) for d in (1, 2, 3)]
    square = shape((2, HW, HW))
    mine, other = local_call(column_kernel, (square, square), (at,), *rows, prefix, first)
    return mine, rotated(other, "c", 1)


def add(a, b):
    return (a.astype(f32) + b.astype(f32)).astype(bf)


def attended_blocks(offsets, me, q, keys, values, w, after=()):
    count = len(offsets)
    ids = jnp.stack([lax.rem(me + o + 8, 8) for o in offsets]).astype(jnp.int32)
    half = shape((RT, HALF))
    outs = local_call(
        functools.partial(attention_kernel, count), (half,) * (2 * count), (ids,),
        q, keys, values, w,
        flops=count * (5 << 29), after=after, mib=26,
        scratch=[
            pltpu.VMEM((2, G * RT, WINDOW), f32),
            pltpu.VMEM((2, G * RT, HW), f32),
            pltpu.VMEM((G * RT, 2 * HW), f32),
            pltpu.VMEM((count * RT, G * HW), bf),
        ])
    return {o: outs[2 * t : 2 * t + 2] for t, o in enumerate(offsets)}


def reduced_rows(me, q, keys, values, w):
    part = attended_blocks((4,), me, q, keys, values, w)
    up = [rotated(part[4][0], "head", 1), None]
    down = [None, rotated(part[4][1], "head", -1)]
    sent = ()
    for k in (3, 2, 1):
        part = attended_blocks((k, -k), me, q, keys, values, w, sent)
        sent = []
        for n in range(2):
            ahead, back = part[k][n], part[-k][n]
            ahead = ahead if up[n] is None else add(up[n], ahead)
            back = back if down[n] is None else add(down[n], back)
            up[n] = rotated(ahead, "head", 1)
            down[n] = rotated(back, "head", -1)
            sent += [ahead, back]
    own = attended_blocks((0,), me, q, keys, values, w, sent)[0]
    return (*up, *down, *own)


def delta_blocks(offsets, me, halves, weights, terms):
    count = len(offsets)
    ids = jnp.stack([lax.rem(me + o + 8, 8) for o in offsets]).astype(jnp.int32)
    return local_call(
        functools.partial(block_kernel, count),
        (shape((count, W4, HW)), shape((count, W4, HW), f32), shape((count, G, HW, 2 * HW))),
        (ids,), *halves, *terms, far=weights, flops=count * (5 << 29), mib=24,
        scratch=[pltpu.VMEM((2 * HALF, 6 * HW), bf), pltpu.SemaphoreType.DMA((KSTEPS, 3))])


def delta_rows(at, a, b, weights, terms):
    me = at[3]
    offsets = [(0,)]
    parts = [*delta_blocks((0,), me, (a, b), weights, terms)]
    up, down = [a, b], [a, b]
    for k in (1, 2, 3):
        up = [rotated(h, "head", 1) for h in up]
        down = [rotated(h, "head", -1) for h in down]
        offsets.append((-k, k))
        parts += delta_blocks((-k, k), me, (*up, *down), weights, terms)
    last = (rotated(up[0], "head", 1), rotated(down[1], "head", -1))
    offsets.append((4,))
    parts += delta_blocks((4,), me, last, weights, terms)
    return local_call(
        functools.partial(chain_kernel, tuple(offsets)),
        (shape((G, HW, 2 * HW)), shape((G, TOK, HW)), shape((TOK, G * HW), f32)),
        (at,), terms[1], *parts, mib=20,
        scratch=[
            pltpu.VMEM((8, W4, HW), bf),
            pltpu.VMEM((8, W4, HW), f32),
            pltpu.VMEM((8, G, HW, 2 * HW), bf),
        ])


def body(
    residual,
    sliding_query_heads,
    sliding_key_heads,
    sliding_value_heads,
    output_weight,
    norm_gain,
    query_weight,
    key_weight,
    value_weight,
    write_strength,
    log_decay,
):
    x, y, c, me = (lax.axis_index(a) for a in SEQ + ("head",))
    at = jnp.stack([x, y, c, me]).astype(jnp.int32)
    shard = (x * lax.axis_size("y") + y) * 2 + c
    low = jnp.maximum(0, (WINDOW // TOK - shard) * TOK).astype(jnp.int32)[None]
    own = jnp.concatenate([sliding_key_heads, sliding_value_heads], axis=1)
    d, odd = earlier_rows(own)
    weights = (query_weight, key_weight, value_weight)
    terms = decay_terms(write_strength, log_decay)
    wide = shape((9 * TOK, 2 * HW))
    keys, values = local_call(
        window_kernel, (wide, wide), (low,), far=(own, d[2], d[4], d[6], d[8], odd), mib=16,
        scratch=[pltpu.SemaphoreType.DMA((9, 2))])
    sums = reduced_rows(me, sliding_query_heads, keys, values, output_weight)
    half = shape((RT, HALF))
    mixed_stream, a, b = local_call(
        norm_kernel, (shape(residual.shape), half, half), (),
        *sums, residual, norm_gain[None, :])
    maps, twisted, local = delta_rows(at, a, b, weights, terms)
    mine, other = incoming_state(at, maps)
    delta_output = local_call(
        readout_kernel, shape((TOK, G * HW)), (at,), mine, other, twisted, local)
    return mixed_stream, delta_output


def solution(mesh):
    devices = mesh.devices.reshape(4, 4, 2, 8)
    split = Mesh(devices, SEQ + ("head",))
    in_specs = (
        P(SEQ + ("head",), None),
        P(SEQ, "head"),
        P(SEQ, "head"),
        P(SEQ, "head"),
        P("head", None),
        P(),
        P(None, "head"),
        P(None, "head"),
        P(None, "head"),
        P("head", SEQ),
        P("head", SEQ),
    )
    out_specs = (P(SEQ + ("head",), None), P(SEQ, "head"))
    return jax.shard_map(body, mesh=split, in_specs=in_specs, out_specs=out_specs, check_vma=False)
```

```python
import functools
import math

import jax
import jax.numpy as jnp
from jax import lax
from jax.experimental import pallas as pl
from jax.experimental.pallas import tpu as pltpu
from jax.sharding import Mesh
from jax.sharding import PartitionSpec as P

bf = jnp.bfloat16
f32 = jnp.float32
HW = 128
G = 4
WINDOW = 4096
TOK = 512
NEG = -1e30
SCALE = math.log2(math.e) / math.sqrt(HW)
RT = 64
HALF = 2048
CK = 4096
C = 64
W4 = G * C
SEQ = ("x", "y", "c")


def join_kernel(a_ref, b_ref, out_ref, sems):
    copies = [
        pltpu.make_async_copy(ref, out_ref.at[:, pl.ds(n * HW, HW)], sems.at[n])
        for n, ref in enumerate((a_ref, b_ref))
    ]
    for copy in copies:
        copy.start()
    for copy in copies:
        copy.wait()


def window_kernel(low_ref, own_ref, d2_ref, d4_ref, d6_ref, d8_ref, odd_ref, keys, values, sems):
    even = {0: own_ref, 2: d2_ref, 4: d4_ref, 6: d6_ref, 8: d8_ref}
    lane = lax.broadcasted_iota(jnp.int32, (TOK, HW), 1)
    copies = []
    for d in range(9):
        rows = pl.ds((8 - d) * TOK, TOK)
        src = even[d] if d in even else odd_ref.at[(d - 1) // 2]
        for n, dst in enumerate((keys, values)):
            copies.append(pltpu.make_async_copy(
                src.at[:, pl.ds(n * HW, HW)], dst.at[rows, pl.ds(0, HW)], sems.at[d, n]))
    for copy in copies:
        copy.start()
    for d in range(9):
        rows = slice((8 - d) * TOK, (9 - d) * TOK)
        bias = jnp.where((8 - d) * TOK < low_ref[0], NEG, 0.0)
        keys[rows, HW:] = jnp.where(lane == 0, bias, 0.0).astype(bf)
        values[rows, HW:] = jnp.ones((TOK, HW), bf)
    for copy in copies:
        copy.wait()


def attention_kernel(count, blocks_ref, q_ref, keys, values, w_ref, *rest):
    outs, (scores, top, acc, att, *own) = rest[: 2 * count], rest[2 * count :]
    if own:
        w_copy = pltpu.make_async_copy(w_ref, own[0], own[1])
        w_copy.start()
        w_ref = own[0]
    r = lax.broadcasted_iota(jnp.int32, (G * RT, HW), 0) % RT
    c = lax.broadcasted_iota(jnp.int32, (G * RT, HW), 1)
    unit = jnp.where(c == 0, 1.0, 0.0).astype(bf)
    steps = WINDOW // CK

    def place(t):
        block = blocks_ref[t]
        half = lax.rem(block, 2)
        return pl.multiple_of((block - half) * RT, 2 * RT), c > r + half * RT

    def queries(t):
        q = q_ref[pl.ds(pl.multiple_of(blocks_ref[t] * RT, RT), RT), :]
        q = jnp.concatenate([q[:, h * HW : (h + 1) * HW] for h in range(G)], axis=0)
        return jnp.concatenate([q, unit], axis=1)

    def dot_t(a, b):
        return lax.dot_general(a, b, (((1,), (1,)), ((), ())), preferred_element_type=f32)

    def columns(j):
        return pl.ds(j * CK if isinstance(j, int) else pl.multiple_of(j * CK, CK), CK)

    def score(t, j):
        base, oldest = place(t)
        q = queries(t)
        s = dot_t(q, keys[pl.ds(pl.multiple_of(base + j * CK, 2 * RT), CK), :])
        first = isinstance(j, int)
        if first:
            newest = dot_t(q, keys[pl.ds(pl.multiple_of(base + WINDOW, 2 * RT), HW), :])
            s = jnp.concatenate([jnp.where(oldest, s[:, :HW], newest), s[:, HW:]], axis=1)
        scores[t % 2, :, columns(j)] = s
        m = functools.reduce(
            jnp.maximum, [s[:, i * HW : (i + 1) * HW] for i in range(CK // HW)])
        top[t % 2] = m if first else jnp.maximum(top[t % 2], m)

    def weigh(t, j, m):
        base, oldest = place(t)
        v = values[pl.ds(pl.multiple_of(base + j * CK, 2 * RT), CK), :]
        s = scores[t % 2, :, columns(j)]
        p = jnp.concatenate(
            [jnp.exp2((s[:, i * HW : (i + 1) * HW] - m) * SCALE) for i in range(CK // HW)], axis=1)
        if isinstance(j, int):
            edge = p[:, :HW]
            old = jnp.where(oldest, edge, 0.0)
            p = jnp.concatenate([old, p[:, HW:], edge - old], axis=1)
            v = jnp.concatenate(
                [v, values[pl.ds(pl.multiple_of(base + WINDOW, 2 * RT), HW), :]], axis=0)
            acc[...] = jnp.dot(p.astype(bf), v, preferred_element_type=f32)
        else:
            acc[...] += jnp.dot(p.astype(bf), v, preferred_element_type=f32)

    def pre(j, _):
        score(0, j)
        return _

    score(0, 0)
    lax.fori_loop(1, steps, pre, 0)
    for t in range(count):
        m = jnp.broadcast_to(jnp.max(top[t % 2], axis=1, keepdims=True), (G * RT, HW))
        top[t % 2] = m
        weigh(t, 0, m)
        if t + 1 < count:
            score(t + 1, 0)

        def step(j, _):
            weigh(t, j, top[t % 2])
            if t + 1 < count:
                score(t + 1, j)
            return _

        lax.fori_loop(1, steps, step, 0)
        a = acc[...]
        o = (a[:, :HW] / a[:, HW:]).astype(bf)
        for h in range(G):
            att[t * RT : (t + 1) * RT, h * HW : (h + 1) * HW] = o[h * RT : (h + 1) * RT]
    if own:
        w_copy.wait()
    for n in range(2):
        part = jnp.dot(
            att[...], w_ref[:, n * HALF : (n + 1) * HALF], preferred_element_type=f32).astype(bf)
        for t in range(count):
            outs[2 * t + n][...] = part[t * RT : (t + 1) * RT]


def mm(a, b):
    return jnp.dot(a.astype(bf), b.astype(bf), preferred_element_type=f32)


def mm_t(a, b):
    return lax.dot_general(
        a.astype(bf), b.astype(bf), (((1,), (1,)), ((), ())), preferred_element_type=f32)


def tmm(a, b):
    return lax.dot_general(
        a.astype(bf), b.astype(bf), (((0,), (0,)), ((), ())), preferred_element_type=f32)


def unit_rows(rows):
    return rows / jnp.sqrt(jnp.sum(rows * rows, axis=1, keepdims=True) + 1e-6)


def block_kernel(count, blocks_ref, *refs):
    pieces = refs[: 2 * count]
    wq_ref, wk_ref, wv_ref, row_ref, col_ref, reduced_ref, local_ref, map_ref = refs[2 * count :]
    a = jnp.concatenate([pieces[2 * t][...] for t in range(count)], axis=0)
    b = jnp.concatenate([pieces[2 * t + 1][...] for t in range(count)], axis=0)
    row = jnp.concatenate([a, b], axis=1)
    lifted = jnp.concatenate(
        [jnp.dot(row, ref[...], preferred_element_type=f32) for ref in (wq_ref, wk_ref, wv_ref)],
        axis=1)
    i = lax.broadcasted_iota(jnp.int32, (W4, W4), 0)
    j = lax.broadcasted_iota(jnp.int32, (W4, W4), 1)
    within = (i >= j) & (i // C == j // C)
    levels = []
    size = 1
    while size < C:
        levels.append((i // (2 * size) == j // (2 * size)) & (i // size != j // size) & (i > j))
        size *= 2
    eye = jnp.where(i == j, 1.0, 0.0).astype(f32)
    sides, scaled, carried, lower, attend = [], [], [], [], []
    for t in range(count):
        rows = lifted[t * C : (t + 1) * C]
        q4 = jnp.concatenate([unit_rows(rows[:, :HW])] * G, axis=0)
        k4 = jnp.concatenate([unit_rows(rows[:, HW : 2 * HW])] * G, axis=0)
        v4 = jnp.concatenate([rows[:, (2 + h) * HW : (3 + h) * HW] for h in range(G)], axis=0)
        col = col_ref[blocks_ref[t]]
        cum, last, strength = col[:, :1], col[:, 1:2], col[:, 2:3]
        ratio = jnp.where(
            within, jnp.exp(jnp.where(within, cum - row_ref[blocks_ref[t]], 0.0)), 0.0)
        lower.append(strength * ratio * mm_t(k4, k4))
        attend.append((mm_t(q4, k4) * ratio).astype(bf))
        growth = jnp.exp(cum)
        sides.append(
            jnp.concatenate([(strength * growth) * k4, strength * v4], axis=1).astype(bf))
        scaled.append(growth * q4)
        carried.append((jnp.exp(last - cum) * k4).astype(bf))
    inverse = [eye - jnp.where(levels[0], low, 0.0) for low in lower]
    for mask in levels[1:]:
        moved = [mm(x, jnp.where(mask, low, 0.0)) for x, low in zip(inverse, lower)]
        inverse = [x - mm(y, x) for x, y in zip(inverse, moved)]
    mixed = [mm(x, side).astype(bf) for x, side in zip(inverse, sides)]
    seen = [mm(near, mix) for near, mix in zip(attend, mixed)]
    for t in range(count):
        reduced_ref[t] = (scaled[t] - seen[t][:, :HW]).astype(bf)
        local_ref[t] = seen[t][:, HW:]
        for h in range(G):
            rows = slice(h * C, (h + 1) * C)
            map_ref[t, h] = tmm(carried[t][rows], mixed[t][rows]).astype(bf)


def chain_kernel(offsets, at_ref, col_ref, *refs):
    n = sum(offsets, ())
    parts, refs = refs[: 3 * len(offsets)], refs[3 * len(offsets) :]
    maps_ref, theirs_ref, twist_ref, out_ref, reduced, local, maps = refs
    blocks = len(n)
    for k, group in enumerate(offsets):
        for t, offset in enumerate(group):
            at = lax.rem(at_ref[3] + offset + blocks, blocks)
            reduced[at] = parts[3 * k][t]
            local[at] = parts[3 * k + 1][t]
            maps[at] = parts[3 * k + 2][t]
    i = lax.broadcasted_iota(jnp.int32, (HW, 2 * HW), 0)
    j = lax.broadcasted_iota(jnp.int32, (HW, 2 * HW), 1)
    state = [jnp.where(i == j, 1.0, 0.0).astype(f32)] * G
    for n in range(blocks):
        for h in range(G):
            rows = slice(h * C, (h + 1) * C)
            m = maps[n, h]
            decay = jnp.exp(col_ref[n, h * C : h * C + 1, 1:2])
            both = mm(jnp.concatenate([reduced[n, rows], m[:, :HW]], axis=0), state[h])
            twist_ref[h, n * C : (n + 1) * C, :] = both[:C, :HW].astype(bf)
            out_ref[n * C : (n + 1) * C, h * HW : (h + 1) * HW] = both[:C, HW:] + local[n, rows]
            state[h] = decay * state[h] - both[C:] + jnp.where(j >= HW, m.astype(f32), 0.0)
    c = at_ref[2]
    for h in range(2):
        low, high = state[h].astype(bf), state[h + 2].astype(bf)
        maps_ref[h] = jnp.where(c == 0, low, high)
        theirs_ref[h] = jnp.where(c == 0, high, low)


def decay_terms(write_strength, log_decay):
    g, rows = log_decay.shape
    blocks = rows // C
    cum = jnp.cumsum(log_decay.reshape(g, blocks, C), axis=-1)
    last = jnp.broadcast_to(cum[:, :, -1:], cum.shape)
    strength = write_strength.reshape(g, blocks, C)
    col = jnp.stack([cum, last, strength], axis=-1).transpose(1, 0, 2, 3)
    return cum.transpose(1, 0, 2).reshape(blocks, 1, g * C), col.reshape(blocks, g * C, 3)


def spread(before, later):
    high = before.astype(bf)
    low = (before - high.astype(f32)).astype(bf)
    m = later[:, :HW]
    return (jnp.dot(m, high, preferred_element_type=f32)
            + jnp.dot(m, low, preferred_element_type=f32))


def with_injected(before, later):
    n = later[:, HW:].astype(f32)
    return spread(before, later) + jnp.concatenate([jnp.zeros_like(n), n], axis=1)


def chip_kernel(at_ref, own_ref, other_ref, first_ref, total_ref):
    c = at_ref[2]
    for h in range(2):
        own, other = own_ref[h], other_ref[h]
        first = jnp.where(c == 0, own, other)
        second = jnp.where(c == 0, other, own)
        first_ref[h] = first
        total_ref[h] = with_injected(first.astype(f32), second).astype(bf)


def row_kernel(at_ref, t0_ref, t1_ref, t2_ref, t3_ref, prefix_ref, total_ref, injected_ref, parts):
    y = at_ref[1]
    for r, t in enumerate((t0_ref, t1_ref, t2_ref, t3_ref)):
        parts[lax.rem(y - r + 4, 4)] = t[...]
    i = lax.broadcasted_iota(jnp.int32, (HW, 2 * HW), 0)
    j = lax.broadcasted_iota(jnp.int32, (HW, 2 * HW), 1)
    start = jnp.where(i == j, 1.0, 0.0).astype(f32)
    for h in range(2):
        now = start
        kept = start
        for k in range(4):
            kept = jnp.where(k == y, now, kept)
            now = with_injected(now, parts[k, h])
        prefix_ref[h] = kept
        total_ref[h] = now.astype(bf)
        injected_ref[h] = now[:, HW:].astype(bf)


def column_kernel(at_ref, x1_ref, x2_ref, x3_ref, prefix_ref, first_ref, mine_ref, other_ref):
    x, c = at_ref[0], at_ref[2]
    for h in range(2):
        state = jnp.zeros((HW, HW), f32)
        for d, t in ((3, x3_ref), (2, x2_ref), (1, x1_ref)):
            if d == 3:
                new = t[h].astype(f32)
            else:
                new = spread(state, t[h]) + t[h, :, HW:].astype(f32)
            state = jnp.where(x >= d, new, state)
        p = prefix_ref[h]
        p_high = p[:, :HW].astype(bf)
        p_low = (p[:, :HW] - p_high.astype(f32)).astype(bf)
        s = state.astype(bf)
        s_low = (state - s.astype(f32)).astype(bf)
        zero = (jnp.dot(p_high, s, preferred_element_type=f32)
                + jnp.dot(p_low, s, preferred_element_type=f32)
                + jnp.dot(p_high, s_low, preferred_element_type=f32) + p[:, HW:])
        one = spread(zero, first_ref[h]) + first_ref[h, :, HW:].astype(f32)
        mine_ref[h] = jnp.where(c == 0, zero, one).astype(bf)
        other_ref[h] = jnp.where(c == 0, one, zero).astype(bf)


def readout_kernel(at_ref, mine_ref, other_ref, twist_ref, local_ref, out_ref):
    c = at_ref[2]
    for h in range(G):
        own = (h // 2) == c
        state = jnp.where(own, mine_ref[h % 2], other_ref[h % 2])
        cols = slice(h * HW, (h + 1) * HW)
        out_ref[:, cols] = (local_ref[:, cols] + jnp.dot(
            twist_ref[h], state, preferred_element_type=f32)).astype(bf)


def norm_kernel(*refs):
    *sums, residual_ref, gain_ref, mixed_ref, a_ref, b_ref = refs
    total = residual_ref[...].astype(f32) + jnp.concatenate(
        [sum(s[...].astype(f32) for s in sums[n::2]) for n in range(2)], axis=1)
    mixed = total.astype(bf)
    mixed_ref[...] = mixed
    stream = mixed.astype(f32)
    scale = lax.rsqrt(jnp.mean(stream * stream, axis=-1, keepdims=True) + 1e-06)
    normed = (stream * scale * gain_ref[...]).astype(bf)
    a_ref[...] = normed[:, :HALF]
    b_ref[...] = normed[:, HALF:]


VM = pl.BlockSpec(memory_space=pltpu.VMEM)
SM = pl.BlockSpec(memory_space=pltpu.SMEM)


def local_call(kernel, shapes, scalars, *arrays, scratch=(), flops=0, after=(), far=(), mib=12):
    if after:
        held = kernel
        spot = len(scalars) + len(arrays) + len(far)

        def kernel(*refs):
            held(*refs[:spot], *refs[spot + len(after) :])

    cost = pl.CostEstimate(flops=flops, bytes_accessed=1 << 20, transcendentals=0)
    return pl.pallas_call(
        kernel,
        cost_estimate=cost if flops else None,
        out_shape=shapes,
        in_specs=[SM] * len(scalars) + [VM] * len(arrays) + [pl.BlockSpec(memory_space=pltpu.HBM)] * len(far)
        + [pl.BlockSpec(memory_space=pl.ANY)] * len(after),
        out_specs=jax.tree.map(lambda _: VM, shapes),
        scratch_shapes=list(scratch),
        compiler_params=pltpu.CompilerParams(vmem_limit_bytes=mib << 20),
    )(*scalars, *arrays, *far, *after)


def shape(dims, kind=bf):
    return jax.ShapeDtypeStruct(dims, kind)


def rotated(array, axis, by):
    n = lax.axis_size(axis)
    return lax.ppermute(array, axis, [(i, (i + by) % n) for i in range(n)])


def shifted(array, axis, by):
    n = lax.axis_size(axis)
    return lax.ppermute(array, axis, [(i, i + by) for i in range(n - by)])


def earlier_rows(own):
    y, c = lax.axis_index("y"), lax.axis_index("c")
    count = lax.axis_size("y")
    above = shifted(own, "x", 1)
    d = {8: above}
    for r in (1, 2, 3):
        d[2 * r] = rotated(jnp.where(y + r >= count, above, own), "y", r)
    odd = jnp.where(
        c == 0,
        jnp.stack([own, d[2], d[4], d[6]]),
        jnp.stack([d[2], d[4], d[6], d[8]]),
    )
    return d, rotated(odd, "c", 1)


def incoming_state(at, maps, theirs):
    theirs = rotated(theirs, "c", 1)
    two = shape((2, HW, 2 * HW))
    first, total = local_call(chip_kernel, (two, two), (at,), maps, theirs)
    parts = [total] + [rotated(total, "y", r) for r in (1, 2, 3)]
    prefix, row, first_row = local_call(
        row_kernel, (shape((2, HW, 2 * HW), f32), two, shape((2, HW, HW))), (at,), *parts,
        scratch=[pltpu.VMEM((4, 2, HW, 2 * HW), bf)],
    )
    rows = [shifted(row, "x", 1), shifted(row, "x", 2), shifted(first_row, "x", 3)]
    square = shape((2, HW, HW))
    mine, other = local_call(column_kernel, (square, square), (at,), *rows, prefix, first)
    return mine, rotated(other, "c", 1)


def add(a, b):
    return (a.astype(f32) + b.astype(f32)).astype(bf)


def attended_blocks(offsets, me, q, keys, values, w, after=(), fetch=False):
    count = len(offsets)
    ids = jnp.stack([lax.rem(me + o + 8, 8) for o in offsets]).astype(jnp.int32)
    half = shape((RT, HALF))
    outs = local_call(
        functools.partial(attention_kernel, count), (half,) * (2 * count), (ids,),
        q, keys, values, *(() if fetch else (w,)), far=(w,) if fetch else (),
        flops=count * (5 << 29), after=after, mib=24,
        scratch=[
            pltpu.VMEM((2, G * RT, WINDOW), f32),
            pltpu.VMEM((2, G * RT, HW), f32),
            pltpu.VMEM((G * RT, 2 * HW), f32),
            pltpu.VMEM((count * RT, G * HW), bf),
        ] + ([pltpu.VMEM(w.shape, bf), pltpu.SemaphoreType.DMA] if fetch else []))
    return {o: outs[2 * t : 2 * t + 2] for t, o in enumerate(offsets)}


def reduced_rows(me, q, keys, values, w):
    part = attended_blocks((4,), me, q, keys, values, w)
    up = [rotated(part[4][0], "head", 1), None]
    down = [None, rotated(part[4][1], "head", -1)]
    sent, own = (), ()
    for k in (3, 2, 1):
        offsets = (k, -k, 0) if k == 2 else (k, -k)
        part = attended_blocks(offsets, me, q, keys, values, w, sent)
        own = part.get(0, ()) if k == 2 else own
        sent = []
        for n in range(2):
            ahead, back = part[k][n], part[-k][n]
            ahead = ahead if up[n] is None else add(up[n], ahead)
            back = back if down[n] is None else add(down[n], back)
            up[n] = rotated(ahead, "head", 1)
            down[n] = rotated(back, "head", -1)
            sent += [ahead, back]
    return (*up, *down, *own)


def delta_blocks(offsets, me, halves, weights, terms):
    count = len(offsets)
    ids = jnp.stack([lax.rem(me + o + 8, 8) for o in offsets]).astype(jnp.int32)
    return local_call(
        functools.partial(block_kernel, count),
        (shape((count, W4, HW)), shape((count, W4, HW), f32), shape((count, G, HW, 2 * HW))),
        (ids,), *halves, *weights, *terms, flops=count * (5 << 29), mib=14)


def delta_rows(at, a, b, weights, terms):
    me = at[3]
    offsets = [(0,)]
    parts = [*delta_blocks((0,), me, (a, b), weights, terms)]
    up, down = [a, b], [a, b]
    for k in (1, 2, 3):
        up = [rotated(h, "head", 1) for h in up]
        down = [rotated(h, "head", -1) for h in down]
        offsets.append((-k, k))
        parts += delta_blocks((-k, k), me, (*up, *down), weights, terms)
    last = (rotated(up[0], "head", 1), rotated(down[1], "head", -1))
    offsets.append((4,))
    parts += delta_blocks((4,), me, last, weights, terms)
    return local_call(
        functools.partial(chain_kernel, tuple(offsets)),
        (shape((2, HW, 2 * HW)),) * 2 + (shape((G, TOK, HW)), shape((TOK, G * HW), f32)),
        (at,), terms[1], *parts, mib=20,
        scratch=[
            pltpu.VMEM((8, W4, HW), bf),
            pltpu.VMEM((8, W4, HW), f32),
            pltpu.VMEM((8, G, HW, 2 * HW), bf),
        ])


def body(
    residual,
    sliding_query_heads,
    sliding_key_heads,
    sliding_value_heads,
    output_weight,
    norm_gain,
    query_weight,
    key_weight,
    value_weight,
    write_strength,
    log_decay,
):
    x, y, c, me = (lax.axis_index(a) for a in SEQ + ("head",))
    at = jnp.stack([x, y, c, me]).astype(jnp.int32)
    shard = (x * lax.axis_size("y") + y) * 2 + c
    low = jnp.maximum(0, (WINDOW // TOK - shard) * TOK).astype(jnp.int32)[None]
    own = local_call(
        join_kernel, shape((TOK, 2 * HW)), (),
        far=(sliding_key_heads, sliding_value_heads), scratch=[pltpu.SemaphoreType.DMA((2,))])
    d, odd = earlier_rows(own)
    weights = (query_weight, key_weight, value_weight)
    terms = decay_terms(write_strength, log_decay)
    wide = shape((9 * TOK, 2 * HW))
    keys, values = local_call(
        window_kernel, (wide, wide), (low,), far=(own, d[2], d[4], d[6], d[8], odd), mib=16,
        scratch=[pltpu.SemaphoreType.DMA((9, 2))])
    sums = reduced_rows(me, sliding_query_heads, keys, values, output_weight)
    half = shape((RT, HALF))
    mixed_stream, a, b = local_call(
        norm_kernel, (shape(residual.shape), half, half), (),
        *sums, residual, norm_gain[None, :])
    maps, theirs, twisted, local = delta_rows(at, a, b, weights, terms)
    mine, other = incoming_state(at, maps, theirs)
    delta_output = local_call(
        readout_kernel, shape((TOK, G * HW)), (at,), mine, other, twisted, local)
    return mixed_stream, delta_output


def solution(mesh):
    devices = mesh.devices.reshape(4, 4, 2, 8)
    split = Mesh(devices, SEQ + ("head",))
    in_specs = (
        P(SEQ + ("head",), None),
        P(SEQ, "head"),
        P(SEQ, "head"),
        P(SEQ, "head"),
        P("head", None),
        P(),
        P(None, "head"),
        P(None, "head"),
        P(None, "head"),
        P("head", SEQ),
        P("head", SEQ),
    )
    out_specs = (P(SEQ + ("head",), None), P(SEQ, "head"))
    return jax.shard_map(body, mesh=split, in_specs=in_specs, out_specs=out_specs, check_vma=False)
```

```python
import functools
import math

import jax
import jax.numpy as jnp
from jax import lax
from jax.experimental import pallas as pl
from jax.experimental.pallas import tpu as pltpu
from jax.sharding import Mesh
from jax.sharding import PartitionSpec as P

bf = jnp.bfloat16
f32 = jnp.float32
HW = 128
G = 4
WINDOW = 4096
TOK = 512
NEG = -1e30
SCALE = math.log2(math.e) / math.sqrt(HW)
RT = 64
HALF = 2048
CK = 4096
C = 64
W4 = G * C
SEQ = ("x", "y", "c")


def join_kernel(a_ref, b_ref, out_ref, sems):
    copies = [
        pltpu.make_async_copy(ref, out_ref.at[:, pl.ds(n * HW, HW)], sems.at[n])
        for n, ref in enumerate((a_ref, b_ref))
    ]
    for copy in copies:
        copy.start()
    for copy in copies:
        copy.wait()


def window_kernel(low_ref, own_ref, d2_ref, d4_ref, d6_ref, d8_ref, odd_ref, keys, values, sems):
    even = {0: own_ref, 2: d2_ref, 4: d4_ref, 6: d6_ref, 8: d8_ref}
    lane = lax.broadcasted_iota(jnp.int32, (TOK, HW), 1)
    copies = []
    for d in range(9):
        rows = pl.ds((8 - d) * TOK, TOK)
        src = even[d] if d in even else odd_ref.at[(d - 1) // 2]
        for n, dst in enumerate((keys, values)):
            copies.append(pltpu.make_async_copy(
                src.at[:, pl.ds(n * HW, HW)], dst.at[rows, pl.ds(0, HW)], sems.at[d, n]))
    for copy in copies:
        copy.start()
    for d in range(9):
        rows = slice((8 - d) * TOK, (9 - d) * TOK)
        bias = jnp.where((8 - d) * TOK < low_ref[0], NEG, 0.0)
        keys[rows, HW:] = jnp.where(lane == 0, bias, 0.0).astype(bf)
        values[rows, HW:] = jnp.ones((TOK, HW), bf)
    for copy in copies:
        copy.wait()


def attention_kernel(count, blocks_ref, q_ref, keys, values, w_ref, *rest):
    outs, (scores, top, acc, att, *own) = rest[: 2 * count], rest[2 * count :]
    if own:
        w_copy = pltpu.make_async_copy(w_ref, own[0], own[1])
        w_copy.start()
        w_ref = own[0]
    r = lax.broadcasted_iota(jnp.int32, (G * RT, HW), 0) % RT
    c = lax.broadcasted_iota(jnp.int32, (G * RT, HW), 1)
    unit = jnp.where(c == 0, 1.0, 0.0).astype(bf)
    steps = WINDOW // CK

    def place(t):
        block = blocks_ref[t]
        half = lax.rem(block, 2)
        return pl.multiple_of((block - half) * RT, 2 * RT), c > r + half * RT

    def queries(t):
        q = q_ref[pl.ds(pl.multiple_of(blocks_ref[t] * RT, RT), RT), :]
        q = jnp.concatenate([q[:, h * HW : (h + 1) * HW] for h in range(G)], axis=0)
        return jnp.concatenate([q, unit], axis=1)

    def dot_t(a, b):
        return lax.dot_general(a, b, (((1,), (1,)), ((), ())), preferred_element_type=f32)

    def columns(j):
        return pl.ds(j * CK if isinstance(j, int) else pl.multiple_of(j * CK, CK), CK)

    def score(t, j):
        base, oldest = place(t)
        q = queries(t)
        s = dot_t(q, keys[pl.ds(pl.multiple_of(base + j * CK, 2 * RT), CK), :])
        first = isinstance(j, int)
        if first:
            newest = dot_t(q, keys[pl.ds(pl.multiple_of(base + WINDOW, 2 * RT), HW), :])
            s = jnp.concatenate([jnp.where(oldest, s[:, :HW], newest), s[:, HW:]], axis=1)
        scores[t % 2, :, columns(j)] = s
        m = functools.reduce(
            jnp.maximum, [s[:, i * HW : (i + 1) * HW] for i in range(CK // HW)])
        top[t % 2] = m if first else jnp.maximum(top[t % 2], m)

    def weigh(t, j, m):
        base, oldest = place(t)
        v = values[pl.ds(pl.multiple_of(base + j * CK, 2 * RT), CK), :]
        s = scores[t % 2, :, columns(j)]
        p = jnp.concatenate(
            [jnp.exp2((s[:, i * HW : (i + 1) * HW] - m) * SCALE) for i in range(CK // HW)], axis=1)
        if isinstance(j, int):
            edge = p[:, :HW]
            old = jnp.where(oldest, edge, 0.0)
            p = jnp.concatenate([old, p[:, HW:], edge - old], axis=1)
            v = jnp.concatenate(
                [v, values[pl.ds(pl.multiple_of(base + WINDOW, 2 * RT), HW), :]], axis=0)
            acc[...] = jnp.dot(p.astype(bf), v, preferred_element_type=f32)
        else:
            acc[...] += jnp.dot(p.astype(bf), v, preferred_element_type=f32)

    def pre(j, _):
        score(0, j)
        return _

    score(0, 0)
    lax.fori_loop(1, steps, pre, 0)
    for t in range(count):
        m = jnp.broadcast_to(jnp.max(top[t % 2], axis=1, keepdims=True), (G * RT, HW))
        top[t % 2] = m
        weigh(t, 0, m)
        if t + 1 < count:
            score(t + 1, 0)

        def step(j, _):
            weigh(t, j, top[t % 2])
            if t + 1 < count:
                score(t + 1, j)
            return _

        lax.fori_loop(1, steps, step, 0)
        a = acc[...]
        o = (a[:, :HW] / a[:, HW:]).astype(bf)
        for h in range(G):
            att[t * RT : (t + 1) * RT, h * HW : (h + 1) * HW] = o[h * RT : (h + 1) * RT]
    if own:
        w_copy.wait()
    for n in range(2):
        part = jnp.dot(
            att[...], w_ref[:, n * HALF : (n + 1) * HALF], preferred_element_type=f32).astype(bf)
        for t in range(count):
            outs[2 * t + n][...] = part[t * RT : (t + 1) * RT]


def mm(a, b):
    return jnp.dot(a.astype(bf), b.astype(bf), preferred_element_type=f32)


def mm_t(a, b):
    return lax.dot_general(
        a.astype(bf), b.astype(bf), (((1,), (1,)), ((), ())), preferred_element_type=f32)


def tmm(a, b):
    return lax.dot_general(
        a.astype(bf), b.astype(bf), (((0,), (0,)), ((), ())), preferred_element_type=f32)


def unit_rows(rows):
    return rows / jnp.sqrt(jnp.sum(rows * rows, axis=1, keepdims=True) + 1e-6)


def block_kernel(count, fetch, blocks_ref, *refs):
    pieces = refs[: 2 * count]
    if fetch:
        row_ref, col_ref, *far, reduced_ref, local_ref, map_ref, sems = refs[2 * count : -3]
        weights = refs[-3:]
        copies = [pltpu.make_async_copy(ref, weights[n], sems.at[n]) for n, ref in enumerate(far)]
        for copy in copies:
            copy.start()
        for copy in copies:
            copy.wait()
    else:
        *weights, row_ref, col_ref, reduced_ref, local_ref, map_ref = refs[2 * count :]
    a = jnp.concatenate([pieces[2 * t][...] for t in range(count)], axis=0)
    b = jnp.concatenate([pieces[2 * t + 1][...] for t in range(count)], axis=0)
    row = jnp.concatenate([a, b], axis=1)
    lifted = jnp.concatenate(
        [jnp.dot(row, ref[...], preferred_element_type=f32) for ref in weights],
        axis=1)
    i = lax.broadcasted_iota(jnp.int32, (W4, W4), 0)
    j = lax.broadcasted_iota(jnp.int32, (W4, W4), 1)
    within = (i >= j) & (i // C == j // C)
    levels = []
    size = 1
    while size < C:
        levels.append((i // (2 * size) == j // (2 * size)) & (i // size != j // size) & (i > j))
        size *= 2
    eye = jnp.where(i == j, 1.0, 0.0).astype(f32)
    sides, scaled, carried, lower, attend = [], [], [], [], []
    for t in range(count):
        rows = lifted[t * C : (t + 1) * C]
        q4 = jnp.concatenate([unit_rows(rows[:, :HW])] * G, axis=0)
        k4 = jnp.concatenate([unit_rows(rows[:, HW : 2 * HW])] * G, axis=0)
        v4 = jnp.concatenate([rows[:, (2 + h) * HW : (3 + h) * HW] for h in range(G)], axis=0)
        col = col_ref[blocks_ref[t]]
        cum, last, strength = col[:, :1], col[:, 1:2], col[:, 2:3]
        ratio = jnp.where(
            within, jnp.exp(jnp.where(within, cum - row_ref[blocks_ref[t]], 0.0)), 0.0)
        lower.append(strength * ratio * mm_t(k4, k4))
        attend.append((mm_t(q4, k4) * ratio).astype(bf))
        growth = jnp.exp(cum)
        sides.append(
            jnp.concatenate([(strength * growth) * k4, strength * v4], axis=1).astype(bf))
        scaled.append(growth * q4)
        carried.append((jnp.exp(last - cum) * k4).astype(bf))
    inverse = [eye - jnp.where(levels[0], low, 0.0) for low in lower]
    for mask in levels[1:]:
        moved = [mm(x, jnp.where(mask, low, 0.0)) for x, low in zip(inverse, lower)]
        inverse = [x - mm(y, x) for x, y in zip(inverse, moved)]
    mixed = [mm(x, side).astype(bf) for x, side in zip(inverse, sides)]
    seen = [mm(near, mix) for near, mix in zip(attend, mixed)]
    for t in range(count):
        reduced_ref[t] = (scaled[t] - seen[t][:, :HW]).astype(bf)
        local_ref[t] = seen[t][:, HW:]
        for h in range(G):
            rows = slice(h * C, (h + 1) * C)
            map_ref[t, h] = tmm(carried[t][rows], mixed[t][rows]).astype(bf)


def chain_kernel(offsets, at_ref, col_ref, *refs):
    n = sum(offsets, ())
    parts, refs = refs[: 3 * len(offsets)], refs[3 * len(offsets) :]
    maps_ref, theirs_ref, twist_ref, out_ref, reduced, local, maps = refs
    blocks = len(n)
    for k, group in enumerate(offsets):
        for t, offset in enumerate(group):
            at = lax.rem(at_ref[3] + offset + blocks, blocks)
            reduced[at] = parts[3 * k][t]
            local[at] = parts[3 * k + 1][t]
            maps[at] = parts[3 * k + 2][t]
    i = lax.broadcasted_iota(jnp.int32, (HW, 2 * HW), 0)
    j = lax.broadcasted_iota(jnp.int32, (HW, 2 * HW), 1)
    state = [jnp.where(i == j, 1.0, 0.0).astype(f32)] * G
    for n in range(blocks):
        for h in range(G):
            rows = slice(h * C, (h + 1) * C)
            m = maps[n, h]
            decay = jnp.exp(col_ref[n, h * C : h * C + 1, 1:2])
            both = mm(jnp.concatenate([reduced[n, rows], m[:, :HW]], axis=0), state[h])
            twist_ref[h, n * C : (n + 1) * C, :] = both[:C, :HW].astype(bf)
            out_ref[n * C : (n + 1) * C, h * HW : (h + 1) * HW] = both[:C, HW:] + local[n, rows]
            state[h] = decay * state[h] - both[C:] + jnp.where(j >= HW, m.astype(f32), 0.0)
    c = at_ref[2]
    for h in range(2):
        low, high = state[h].astype(bf), state[h + 2].astype(bf)
        maps_ref[h] = jnp.where(c == 0, low, high)
        theirs_ref[h] = jnp.where(c == 0, high, low)


def decay_terms(write_strength, log_decay):
    g, rows = log_decay.shape
    blocks = rows // C
    cum = jnp.cumsum(log_decay.reshape(g, blocks, C), axis=-1)
    last = jnp.broadcast_to(cum[:, :, -1:], cum.shape)
    strength = write_strength.reshape(g, blocks, C)
    col = jnp.stack([cum, last, strength], axis=-1).transpose(1, 0, 2, 3)
    return cum.transpose(1, 0, 2).reshape(blocks, 1, g * C), col.reshape(blocks, g * C, 3)


def spread(before, later):
    high = before.astype(bf)
    low = (before - high.astype(f32)).astype(bf)
    m = later[:, :HW]
    return (jnp.dot(m, high, preferred_element_type=f32)
            + jnp.dot(m, low, preferred_element_type=f32))


def with_injected(before, later):
    n = later[:, HW:].astype(f32)
    return spread(before, later) + jnp.concatenate([jnp.zeros_like(n), n], axis=1)


def chip_kernel(at_ref, own_ref, other_ref, first_ref, total_ref):
    c = at_ref[2]
    for h in range(2):
        own, other = own_ref[h], other_ref[h]
        first = jnp.where(c == 0, own, other)
        second = jnp.where(c == 0, other, own)
        first_ref[h] = first
        total_ref[h] = with_injected(first.astype(f32), second).astype(bf)


def row_kernel(at_ref, t0_ref, t1_ref, t2_ref, t3_ref, prefix_ref, total_ref, injected_ref, parts):
    y = at_ref[1]
    for r, t in enumerate((t0_ref, t1_ref, t2_ref, t3_ref)):
        parts[lax.rem(y - r + 4, 4)] = t[...]
    i = lax.broadcasted_iota(jnp.int32, (HW, 2 * HW), 0)
    j = lax.broadcasted_iota(jnp.int32, (HW, 2 * HW), 1)
    start = jnp.where(i == j, 1.0, 0.0).astype(f32)
    for h in range(2):
        now = start
        kept = start
        for k in range(4):
            kept = jnp.where(k == y, now, kept)
            now = with_injected(now, parts[k, h])
        prefix_ref[h] = kept
        total_ref[h] = now.astype(bf)
        injected_ref[h] = now[:, HW:].astype(bf)


def column_kernel(at_ref, x1_ref, x2_ref, x3_ref, prefix_ref, first_ref, mine_ref, other_ref):
    x, c = at_ref[0], at_ref[2]
    for h in range(2):
        state = jnp.zeros((HW, HW), f32)
        for d, t in ((3, x3_ref), (2, x2_ref), (1, x1_ref)):
            if d == 3:
                new = t[h].astype(f32)
            else:
                new = spread(state, t[h]) + t[h, :, HW:].astype(f32)
            state = jnp.where(x >= d, new, state)
        p = prefix_ref[h]
        p_high = p[:, :HW].astype(bf)
        p_low = (p[:, :HW] - p_high.astype(f32)).astype(bf)
        s = state.astype(bf)
        s_low = (state - s.astype(f32)).astype(bf)
        zero = (jnp.dot(p_high, s, preferred_element_type=f32)
                + jnp.dot(p_low, s, preferred_element_type=f32)
                + jnp.dot(p_high, s_low, preferred_element_type=f32) + p[:, HW:])
        one = spread(zero, first_ref[h]) + first_ref[h, :, HW:].astype(f32)
        mine_ref[h] = jnp.where(c == 0, zero, one).astype(bf)
        other_ref[h] = jnp.where(c == 0, one, zero).astype(bf)


def readout_kernel(at_ref, mine_ref, other_ref, twist_ref, local_ref, out_ref):
    c = at_ref[2]
    for h in range(G):
        own = (h // 2) == c
        state = jnp.where(own, mine_ref[h % 2], other_ref[h % 2])
        cols = slice(h * HW, (h + 1) * HW)
        out_ref[:, cols] = (local_ref[:, cols] + jnp.dot(
            twist_ref[h], state, preferred_element_type=f32)).astype(bf)


def norm_kernel(*refs):
    *sums, residual_ref, gain_ref, mixed_ref, a_ref, b_ref = refs
    total = residual_ref[...].astype(f32) + jnp.concatenate(
        [sum(s[...].astype(f32) for s in sums[n::2]) for n in range(2)], axis=1)
    mixed = total.astype(bf)
    mixed_ref[...] = mixed
    stream = mixed.astype(f32)
    scale = lax.rsqrt(jnp.mean(stream * stream, axis=-1, keepdims=True) + 1e-06)
    normed = (stream * scale * gain_ref[...]).astype(bf)
    a_ref[...] = normed[:, :HALF]
    b_ref[...] = normed[:, HALF:]


VM = pl.BlockSpec(memory_space=pltpu.VMEM)
SM = pl.BlockSpec(memory_space=pltpu.SMEM)


def local_call(kernel, shapes, scalars, *arrays, scratch=(), flops=0, after=(), far=(), mib=12):
    if after:
        held = kernel
        spot = len(scalars) + len(arrays) + len(far)

        def kernel(*refs):
            held(*refs[:spot], *refs[spot + len(after) :])

    cost = pl.CostEstimate(flops=flops, bytes_accessed=1 << 20, transcendentals=0)
    return pl.pallas_call(
        kernel,
        cost_estimate=cost if flops else None,
        out_shape=shapes,
        in_specs=[SM] * len(scalars) + [VM] * len(arrays) + [pl.BlockSpec(memory_space=pltpu.HBM)] * len(far)
        + [pl.BlockSpec(memory_space=pl.ANY)] * len(after),
        out_specs=jax.tree.map(lambda _: VM, shapes),
        scratch_shapes=list(scratch),
        compiler_params=pltpu.CompilerParams(vmem_limit_bytes=mib << 20),
    )(*scalars, *arrays, *far, *after)


def shape(dims, kind=bf):
    return jax.ShapeDtypeStruct(dims, kind)


def rotated(array, axis, by):
    n = lax.axis_size(axis)
    return lax.ppermute(array, axis, [(i, (i + by) % n) for i in range(n)])


def shifted(array, axis, by):
    n = lax.axis_size(axis)
    return lax.ppermute(array, axis, [(i, i + by) for i in range(n - by)])


def earlier_rows(own):
    y, c = lax.axis_index("y"), lax.axis_index("c")
    count = lax.axis_size("y")
    above = shifted(own, "x", 1)
    d = {8: above}
    for r in (1, 2, 3):
        d[2 * r] = rotated(jnp.where(y + r >= count, above, own), "y", r)
    odd = jnp.where(
        c == 0,
        jnp.stack([own, d[2], d[4], d[6]]),
        jnp.stack([d[2], d[4], d[6], d[8]]),
    )
    return d, rotated(odd, "c", 1)


def incoming_state(at, maps, theirs):
    theirs = rotated(theirs, "c", 1)
    two = shape((2, HW, 2 * HW))
    first, total = local_call(chip_kernel, (two, two), (at,), maps, theirs)
    parts = [total] + [rotated(total, "y", r) for r in (1, 2, 3)]
    prefix, row, first_row = local_call(
        row_kernel, (shape((2, HW, 2 * HW), f32), two, shape((2, HW, HW))), (at,), *parts,
        scratch=[pltpu.VMEM((4, 2, HW, 2 * HW), bf)],
    )
    rows = [shifted(row, "x", 1), shifted(row, "x", 2), shifted(first_row, "x", 3)]
    square = shape((2, HW, HW))
    mine, other = local_call(column_kernel, (square, square), (at,), *rows, prefix, first)
    return mine, rotated(other, "c", 1)


def add(a, b):
    return (a.astype(f32) + b.astype(f32)).astype(bf)


def attended_blocks(offsets, me, q, keys, values, w, after=(), fetch=False):
    count = len(offsets)
    ids = jnp.stack([lax.rem(me + o + 8, 8) for o in offsets]).astype(jnp.int32)
    half = shape((RT, HALF))
    outs = local_call(
        functools.partial(attention_kernel, count), (half,) * (2 * count), (ids,),
        q, keys, values, *(() if fetch else (w,)), far=(w,) if fetch else (),
        flops=count * (5 << 29), after=after, mib=47 if fetch else 24,
        scratch=[
            pltpu.VMEM((2, G * RT, WINDOW), f32),
            pltpu.VMEM((2, G * RT, HW), f32),
            pltpu.VMEM((G * RT, 2 * HW), f32),
            pltpu.VMEM((count * RT, G * HW), bf),
        ] + ([pltpu.VMEM(w.shape, bf), pltpu.SemaphoreType.DMA] if fetch else []))
    return {o: outs[2 * t : 2 * t + 2] for t, o in enumerate(offsets)}


def reduced_rows(me, q, keys, values, w):
    part = attended_blocks((4,), me, q, keys, values, w, fetch=True)
    up = [rotated(part[4][0], "head", 1), None]
    down = [None, rotated(part[4][1], "head", -1)]
    sent, own = (), ()
    for k in (3, 2, 1):
        offsets = (k, -k, 0) if k == 2 else (k, -k)
        part = attended_blocks(offsets, me, q, keys, values, w, sent)
        own = part.get(0, ()) if k == 2 else own
        sent = []
        for n in range(2):
            ahead, back = part[k][n], part[-k][n]
            ahead = ahead if up[n] is None else add(up[n], ahead)
            back = back if down[n] is None else add(down[n], back)
            up[n] = rotated(ahead, "head", 1)
            down[n] = rotated(back, "head", -1)
            sent += [ahead, back]
    return (*up, *down, *own)


def delta_blocks(offsets, me, halves, weights, terms, fetch=False):
    count = len(offsets)
    ids = jnp.stack([lax.rem(me + o + 8, 8) for o in offsets]).astype(jnp.int32)
    return local_call(
        functools.partial(block_kernel, count, fetch),
        (shape((count, W4, HW)), shape((count, W4, HW), f32), shape((count, G, HW, 2 * HW))),
        (ids,), *halves, *(() if fetch else weights), *terms, far=weights if fetch else (),
        flops=count * (5 << 29), mib=52 if fetch else 14,
        scratch=[pltpu.SemaphoreType.DMA((3,))] + [pltpu.VMEM(w.shape, bf) for w in weights]
        if fetch else [])


def delta_rows(at, a, b, weights, terms):
    me = at[3]
    offsets = [(0,)]
    parts = [*delta_blocks((0,), me, (a, b), weights, terms, fetch=True)]
    up, down = [a, b], [a, b]
    for k in (1, 2, 3):
        up = [rotated(h, "head", 1) for h in up]
        down = [rotated(h, "head", -1) for h in down]
        offsets.append((-k, k))
        parts += delta_blocks((-k, k), me, (*up, *down), weights, terms)
    last = (rotated(up[0], "head", 1), rotated(down[1], "head", -1))
    offsets.append((4,))
    parts += delta_blocks((4,), me, last, weights, terms)
    return local_call(
        functools.partial(chain_kernel, tuple(offsets)),
        (shape((2, HW, 2 * HW)),) * 2 + (shape((G, TOK, HW)), shape((TOK, G * HW), f32)),
        (at,), terms[1], *parts, mib=20,
        scratch=[
            pltpu.VMEM((8, W4, HW), bf),
            pltpu.VMEM((8, W4, HW), f32),
            pltpu.VMEM((8, G, HW, 2 * HW), bf),
        ])


def body(
    residual,
    sliding_query_heads,
    sliding_key_heads,
    sliding_value_heads,
    output_weight,
    norm_gain,
    query_weight,
    key_weight,
    value_weight,
    write_strength,
    log_decay,
):
    x, y, c, me = (lax.axis_index(a) for a in SEQ + ("head",))
    at = jnp.stack([x, y, c, me]).astype(jnp.int32)
    shard = (x * lax.axis_size("y") + y) * 2 + c
    low = jnp.maximum(0, (WINDOW // TOK - shard) * TOK).astype(jnp.int32)[None]
    own = local_call(
        join_kernel, shape((TOK, 2 * HW)), (),
        far=(sliding_key_heads, sliding_value_heads), scratch=[pltpu.SemaphoreType.DMA((2,))])
    d, odd = earlier_rows(own)
    weights = (query_weight, key_weight, value_weight)
    terms = decay_terms(write_strength, log_decay)
    wide = shape((9 * TOK, 2 * HW))
    keys, values = local_call(
        window_kernel, (wide, wide), (low,), far=(own, d[2], d[4], d[6], d[8], odd), mib=16,
        scratch=[pltpu.SemaphoreType.DMA((9, 2))])
    sums = reduced_rows(me, sliding_query_heads, keys, values, output_weight)
    half = shape((RT, HALF))
    mixed_stream, a, b = local_call(
        norm_kernel, (shape(residual.shape), half, half), (),
        *sums, residual, norm_gain[None, :])
    maps, theirs, twisted, local = delta_rows(at, a, b, weights, terms)
    mine, other = incoming_state(at, maps, theirs)
    delta_output = local_call(
        readout_kernel, shape((TOK, G * HW)), (at,), mine, other, twisted, local)
    return mixed_stream, delta_output


def solution(mesh):
    devices = mesh.devices.reshape(4, 4, 2, 8)
    split = Mesh(devices, SEQ + ("head",))
    in_specs = (
        P(SEQ + ("head",), None),
        P(SEQ, "head"),
        P(SEQ, "head"),
        P(SEQ, "head"),
        P("head", None),
        P(),
        P(None, "head"),
        P(None, "head"),
        P(None, "head"),
        P("head", SEQ),
        P("head", SEQ),
    )
    out_specs = (P(SEQ + ("head",), None), P(SEQ, "head"))
    return jax.shard_map(body, mesh=split, in_specs=in_specs, out_specs=out_specs, check_vma=False)
```

```python
import functools
import math

import jax
import jax.numpy as jnp
from jax import lax
from jax.experimental import pallas as pl
from jax.experimental.pallas import tpu as pltpu
from jax.sharding import Mesh
from jax.sharding import PartitionSpec as P

bf = jnp.bfloat16
f32 = jnp.float32
HW = 128
G = 4
WINDOW = 4096
TOK = 512
NEG = -1e30
SCALE = math.log2(math.e) / math.sqrt(HW)
RT = 64
HALF = 2048
CK = 4096
C = 64
W4 = G * C
SEQ = ("x", "y", "c")


def join_kernel(a_ref, b_ref, out_ref, sems):
    copies = [
        pltpu.make_async_copy(ref, out_ref.at[:, pl.ds(n * HW, HW)], sems.at[n])
        for n, ref in enumerate((a_ref, b_ref))
    ]
    for copy in copies:
        copy.start()
    for copy in copies:
        copy.wait()


def weights_kernel(q_ref, k_ref, v_ref, out_ref, sems):
    copies = []
    at = 0
    for n, ref in enumerate((q_ref, k_ref, v_ref)):
        width = ref.shape[1]
        copies.append(
            pltpu.make_async_copy(ref, out_ref.at[:, pl.ds(at, width)], sems.at[n]))
        at += width
    for copy in copies:
        copy.start()
    for copy in copies:
        copy.wait()


def window_kernel(low_ref, own_ref, d2_ref, d4_ref, d6_ref, d8_ref, odd_ref, keys, values, sems):
    even = {0: own_ref, 2: d2_ref, 4: d4_ref, 6: d6_ref, 8: d8_ref}
    lane = lax.broadcasted_iota(jnp.int32, (TOK, HW), 1)
    copies = []
    for d in range(9):
        rows = pl.ds((8 - d) * TOK, TOK)
        src = even[d] if d in even else odd_ref.at[(d - 1) // 2]
        for n, dst in enumerate((keys, values)):
            copies.append(pltpu.make_async_copy(
                src.at[:, pl.ds(n * HW, HW)], dst.at[rows, pl.ds(0, HW)], sems.at[d, n]))
    for copy in copies:
        copy.start()
    for d in range(9):
        rows = slice((8 - d) * TOK, (9 - d) * TOK)
        bias = jnp.where((8 - d) * TOK < low_ref[0], NEG, 0.0)
        keys[rows, HW:] = jnp.where(lane == 0, bias, 0.0).astype(bf)
        values[rows, HW:] = jnp.ones((TOK, HW), bf)
    for copy in copies:
        copy.wait()


def attention_kernel(count, blocks_ref, q_ref, keys, values, w_ref, *rest):
    outs, (scores, top, acc, att, *own) = rest[: 2 * count], rest[2 * count :]
    if own:
        w_copy = pltpu.make_async_copy(w_ref, own[0], own[1])
        w_copy.start()
        w_ref = own[0]
    r = lax.broadcasted_iota(jnp.int32, (G * RT, HW), 0) % RT
    c = lax.broadcasted_iota(jnp.int32, (G * RT, HW), 1)
    unit = jnp.where(c == 0, 1.0, 0.0).astype(bf)
    steps = WINDOW // CK

    def place(t):
        block = blocks_ref[t]
        half = lax.rem(block, 2)
        return pl.multiple_of((block - half) * RT, 2 * RT), c > r + half * RT

    def queries(t):
        q = q_ref[pl.ds(pl.multiple_of(blocks_ref[t] * RT, RT), RT), :]
        q = jnp.concatenate([q[:, h * HW : (h + 1) * HW] for h in range(G)], axis=0)
        return jnp.concatenate([q, unit], axis=1)

    def dot_t(a, b):
        return lax.dot_general(a, b, (((1,), (1,)), ((), ())), preferred_element_type=f32)

    def columns(j):
        return pl.ds(j * CK if isinstance(j, int) else pl.multiple_of(j * CK, CK), CK)

    def score(t, j):
        base, oldest = place(t)
        q = queries(t)
        s = dot_t(q, keys[pl.ds(pl.multiple_of(base + j * CK, 2 * RT), CK), :])
        first = isinstance(j, int)
        if first:
            newest = dot_t(q, keys[pl.ds(pl.multiple_of(base + WINDOW, 2 * RT), HW), :])
            s = jnp.concatenate([jnp.where(oldest, s[:, :HW], newest), s[:, HW:]], axis=1)
        scores[t % 2, :, columns(j)] = s
        m = functools.reduce(
            jnp.maximum, [s[:, i * HW : (i + 1) * HW] for i in range(CK // HW)])
        top[t % 2] = m if first else jnp.maximum(top[t % 2], m)

    def weigh(t, j, m):
        base, oldest = place(t)
        v = values[pl.ds(pl.multiple_of(base + j * CK, 2 * RT), CK), :]
        s = scores[t % 2, :, columns(j)]
        p = jnp.concatenate(
            [jnp.exp2((s[:, i * HW : (i + 1) * HW] - m) * SCALE) for i in range(CK // HW)], axis=1)
        if isinstance(j, int):
            edge = p[:, :HW]
            old = jnp.where(oldest, edge, 0.0)
            p = jnp.concatenate([old, p[:, HW:], edge - old], axis=1)
            v = jnp.concatenate(
                [v, values[pl.ds(pl.multiple_of(base + WINDOW, 2 * RT), HW), :]], axis=0)
            acc[...] = jnp.dot(p.astype(bf), v, preferred_element_type=f32)
        else:
            acc[...] += jnp.dot(p.astype(bf), v, preferred_element_type=f32)

    def pre(j, _):
        score(0, j)
        return _

    score(0, 0)
    lax.fori_loop(1, steps, pre, 0)
    for t in range(count):
        m = jnp.broadcast_to(jnp.max(top[t % 2], axis=1, keepdims=True), (G * RT, HW))
        top[t % 2] = m
        weigh(t, 0, m)
        if t + 1 < count:
            score(t + 1, 0)

        def step(j, _):
            weigh(t, j, top[t % 2])
            if t + 1 < count:
                score(t + 1, j)
            return _

        lax.fori_loop(1, steps, step, 0)
        a = acc[...]
        o = (a[:, :HW] / a[:, HW:]).astype(bf)
        for h in range(G):
            att[t * RT : (t + 1) * RT, h * HW : (h + 1) * HW] = o[h * RT : (h + 1) * RT]
    if own:
        w_copy.wait()
    for n in range(2):
        part = jnp.dot(
            att[...], w_ref[:, n * HALF : (n + 1) * HALF], preferred_element_type=f32).astype(bf)
        for t in range(count):
            outs[2 * t + n][...] = part[t * RT : (t + 1) * RT]


def mm(a, b):
    return jnp.dot(a.astype(bf), b.astype(bf), preferred_element_type=f32)


def mm_t(a, b):
    return lax.dot_general(
        a.astype(bf), b.astype(bf), (((1,), (1,)), ((), ())), preferred_element_type=f32)


def tmm(a, b):
    return lax.dot_general(
        a.astype(bf), b.astype(bf), (((0,), (0,)), ((), ())), preferred_element_type=f32)


def unit_rows(rows):
    return rows / jnp.sqrt(jnp.sum(rows * rows, axis=1, keepdims=True) + 1e-6)


def block_kernel(count, blocks_ref, *refs):
    pieces = refs[: 2 * count]
    w_ref, row_ref, col_ref, reduced_ref, local_ref, map_ref = refs[2 * count :]
    a = jnp.concatenate([pieces[2 * t][...] for t in range(count)], axis=0)
    b = jnp.concatenate([pieces[2 * t + 1][...] for t in range(count)], axis=0)
    row = jnp.concatenate([a, b], axis=1)
    lifted = jnp.dot(row, w_ref[...], preferred_element_type=f32)
    i = lax.broadcasted_iota(jnp.int32, (W4, W4), 0)
    j = lax.broadcasted_iota(jnp.int32, (W4, W4), 1)
    within = (i >= j) & (i // C == j // C)
    levels = []
    size = 1
    while size < C:
        levels.append((i // (2 * size) == j // (2 * size)) & (i // size != j // size) & (i > j))
        size *= 2
    eye = jnp.where(i == j, 1.0, 0.0).astype(f32)
    sides, scaled, carried, lower, attend = [], [], [], [], []
    for t in range(count):
        rows = lifted[t * C : (t + 1) * C]
        q4 = jnp.concatenate([unit_rows(rows[:, :HW])] * G, axis=0)
        k4 = jnp.concatenate([unit_rows(rows[:, HW : 2 * HW])] * G, axis=0)
        v4 = jnp.concatenate([rows[:, (2 + h) * HW : (3 + h) * HW] for h in range(G)], axis=0)
        col = col_ref[blocks_ref[t]]
        cum, last, strength = col[:, :1], col[:, 1:2], col[:, 2:3]
        ratio = jnp.where(
            within, jnp.exp(jnp.where(within, cum - row_ref[blocks_ref[t]], 0.0)), 0.0)
        lower.append(strength * ratio * mm_t(k4, k4))
        attend.append((mm_t(q4, k4) * ratio).astype(bf))
        growth = jnp.exp(cum)
        sides.append(
            jnp.concatenate([(strength * growth) * k4, strength * v4], axis=1).astype(bf))
        scaled.append(growth * q4)
        carried.append((jnp.exp(last - cum) * k4).astype(bf))
    inverse = [eye - jnp.where(levels[0], low, 0.0) for low in lower]
    for mask in levels[1:]:
        moved = [mm(x, jnp.where(mask, low, 0.0)) for x, low in zip(inverse, lower)]
        inverse = [x - mm(y, x) for x, y in zip(inverse, moved)]
    mixed = [mm(x, side).astype(bf) for x, side in zip(inverse, sides)]
    seen = [mm(near, mix) for near, mix in zip(attend, mixed)]
    for t in range(count):
        reduced_ref[t] = (scaled[t] - seen[t][:, :HW]).astype(bf)
        local_ref[t] = seen[t][:, HW:]
        for h in range(G):
            rows = slice(h * C, (h + 1) * C)
            map_ref[t, h] = tmm(carried[t][rows], mixed[t][rows]).astype(bf)


def chain_kernel(offsets, at_ref, col_ref, *refs):
    n = sum(offsets, ())
    parts, refs = refs[: 3 * len(offsets)], refs[3 * len(offsets) :]
    maps_ref, theirs_ref, twist_ref, out_ref, reduced, local, maps = refs
    blocks = len(n)
    for k, group in enumerate(offsets):
        for t, offset in enumerate(group):
            at = lax.rem(at_ref[3] + offset + blocks, blocks)
            reduced[at] = parts[3 * k][t]
            local[at] = parts[3 * k + 1][t]
            maps[at] = parts[3 * k + 2][t]
    i = lax.broadcasted_iota(jnp.int32, (HW, 2 * HW), 0)
    j = lax.broadcasted_iota(jnp.int32, (HW, 2 * HW), 1)
    state = [jnp.where(i == j, 1.0, 0.0).astype(f32)] * G
    for n in range(blocks):
        for h in range(G):
            rows = slice(h * C, (h + 1) * C)
            m = maps[n, h]
            decay = jnp.exp(col_ref[n, h * C : h * C + 1, 1:2])
            both = mm(jnp.concatenate([reduced[n, rows], m[:, :HW]], axis=0), state[h])
            twist_ref[h, n * C : (n + 1) * C, :] = both[:C, :HW].astype(bf)
            out_ref[n * C : (n + 1) * C, h * HW : (h + 1) * HW] = both[:C, HW:] + local[n, rows]
            state[h] = decay * state[h] - both[C:] + jnp.where(j >= HW, m.astype(f32), 0.0)
    c = at_ref[2]
    for h in range(2):
        low, high = state[h].astype(bf), state[h + 2].astype(bf)
        maps_ref[h] = jnp.where(c == 0, low, high)
        theirs_ref[h] = jnp.where(c == 0, high, low)


def decay_terms(write_strength, log_decay):
    g, rows = log_decay.shape
    blocks = rows // C
    cum = jnp.cumsum(log_decay.reshape(g, blocks, C), axis=-1)
    last = jnp.broadcast_to(cum[:, :, -1:], cum.shape)
    strength = write_strength.reshape(g, blocks, C)
    col = jnp.stack([cum, last, strength], axis=-1).transpose(1, 0, 2, 3)
    return cum.transpose(1, 0, 2).reshape(blocks, 1, g * C), col.reshape(blocks, g * C, 3)


def spread(before, later):
    high = before.astype(bf)
    low = (before - high.astype(f32)).astype(bf)
    m = later[:, :HW]
    return (jnp.dot(m, high, preferred_element_type=f32)
            + jnp.dot(m, low, preferred_element_type=f32))


def with_injected(before, later):
    n = later[:, HW:].astype(f32)
    return spread(before, later) + jnp.concatenate([jnp.zeros_like(n), n], axis=1)


def chip_kernel(at_ref, own_ref, other_ref, first_ref, total_ref):
    c = at_ref[2]
    for h in range(2):
        own, other = own_ref[h], other_ref[h]
        first = jnp.where(c == 0, own, other)
        second = jnp.where(c == 0, other, own)
        first_ref[h] = first
        total_ref[h] = with_injected(first.astype(f32), second).astype(bf)


def row_kernel(at_ref, t0_ref, t1_ref, t2_ref, t3_ref, prefix_ref, total_ref, injected_ref, parts):
    y = at_ref[1]
    for r, t in enumerate((t0_ref, t1_ref, t2_ref, t3_ref)):
        parts[lax.rem(y - r + 4, 4)] = t[...]
    i = lax.broadcasted_iota(jnp.int32, (HW, 2 * HW), 0)
    j = lax.broadcasted_iota(jnp.int32, (HW, 2 * HW), 1)
    start = jnp.where(i == j, 1.0, 0.0).astype(f32)
    for h in range(2):
        now = start
        kept = start
        for k in range(4):
            kept = jnp.where(k == y, now, kept)
            now = with_injected(now, parts[k, h])
        prefix_ref[h] = kept
        total_ref[h] = now.astype(bf)
        injected_ref[h] = now[:, HW:].astype(bf)


def column_kernel(at_ref, x1_ref, x2_ref, x3_ref, prefix_ref, first_ref, mine_ref, other_ref):
    x, c = at_ref[0], at_ref[2]
    for h in range(2):
        state = jnp.zeros((HW, HW), f32)
        for d, t in ((3, x3_ref), (2, x2_ref), (1, x1_ref)):
            if d == 3:
                new = t[h].astype(f32)
            else:
                new = spread(state, t[h]) + t[h, :, HW:].astype(f32)
            state = jnp.where(x >= d, new, state)
        p = prefix_ref[h]
        p_high = p[:, :HW].astype(bf)
        p_low = (p[:, :HW] - p_high.astype(f32)).astype(bf)
        s = state.astype(bf)
        s_low = (state - s.astype(f32)).astype(bf)
        zero = (jnp.dot(p_high, s, preferred_element_type=f32)
                + jnp.dot(p_low, s, preferred_element_type=f32)
                + jnp.dot(p_high, s_low, preferred_element_type=f32) + p[:, HW:])
        one = spread(zero, first_ref[h]) + first_ref[h, :, HW:].astype(f32)
        mine_ref[h] = jnp.where(c == 0, zero, one).astype(bf)
        other_ref[h] = jnp.where(c == 0, one, zero).astype(bf)


def readout_kernel(at_ref, mine_ref, other_ref, twist_ref, local_ref, out_ref):
    c = at_ref[2]
    for h in range(G):
        own = (h // 2) == c
        state = jnp.where(own, mine_ref[h % 2], other_ref[h % 2])
        cols = slice(h * HW, (h + 1) * HW)
        out_ref[:, cols] = (local_ref[:, cols] + jnp.dot(
            twist_ref[h], state, preferred_element_type=f32)).astype(bf)


def norm_kernel(*refs):
    *sums, residual_ref, gain_ref, mixed_ref, a_ref, b_ref = refs
    total = residual_ref[...].astype(f32) + jnp.concatenate(
        [sum(s[...].astype(f32) for s in sums[n::2]) for n in range(2)], axis=1)
    mixed = total.astype(bf)
    mixed_ref[...] = mixed
    stream = mixed.astype(f32)
    scale = lax.rsqrt(jnp.mean(stream * stream, axis=-1, keepdims=True) + 1e-06)
    normed = (stream * scale * gain_ref[...]).astype(bf)
    a_ref[...] = normed[:, :HALF]
    b_ref[...] = normed[:, HALF:]


VM = pl.BlockSpec(memory_space=pltpu.VMEM)
SM = pl.BlockSpec(memory_space=pltpu.SMEM)


def local_call(kernel, shapes, scalars, *arrays, scratch=(), flops=0, after=(), far=(), mib=12):
    if after:
        held = kernel
        spot = len(scalars) + len(arrays) + len(far)

        def kernel(*refs):
            held(*refs[:spot], *refs[spot + len(after) :])

    cost = pl.CostEstimate(flops=flops, bytes_accessed=1 << 20, transcendentals=0)
    return pl.pallas_call(
        kernel,
        cost_estimate=cost if flops else None,
        out_shape=shapes,
        in_specs=[SM] * len(scalars) + [VM] * len(arrays) + [pl.BlockSpec(memory_space=pltpu.HBM)] * len(far)
        + [pl.BlockSpec(memory_space=pl.ANY)] * len(after),
        out_specs=jax.tree.map(lambda _: VM, shapes),
        scratch_shapes=list(scratch),
        compiler_params=pltpu.CompilerParams(vmem_limit_bytes=mib << 20),
    )(*scalars, *arrays, *far, *after)


def shape(dims, kind=bf):
    return jax.ShapeDtypeStruct(dims, kind)


def rotated(array, axis, by):
    n = lax.axis_size(axis)
    return lax.ppermute(array, axis, [(i, (i + by) % n) for i in range(n)])


def shifted(array, axis, by):
    n = lax.axis_size(axis)
    return lax.ppermute(array, axis, [(i, i + by) for i in range(n - by)])


def earlier_rows(own):
    y, c = lax.axis_index("y"), lax.axis_index("c")
    count = lax.axis_size("y")
    above = shifted(own, "x", 1)
    d = {8: above}
    for r in (1, 2, 3):
        d[2 * r] = rotated(jnp.where(y + r >= count, above, own), "y", r)
    odd = jnp.where(
        c == 0,
        jnp.stack([own, d[2], d[4], d[6]]),
        jnp.stack([d[2], d[4], d[6], d[8]]),
    )
    return d, rotated(odd, "c", 1)


def incoming_state(at, maps, theirs):
    theirs = rotated(theirs, "c", 1)
    two = shape((2, HW, 2 * HW))
    first, total = local_call(chip_kernel, (two, two), (at,), maps, theirs)
    parts = [total] + [rotated(total, "y", r) for r in (1, 2, 3)]
    prefix, row, first_row = local_call(
        row_kernel, (shape((2, HW, 2 * HW), f32), two, shape((2, HW, HW))), (at,), *parts,
        scratch=[pltpu.VMEM((4, 2, HW, 2 * HW), bf)],
    )
    rows = [shifted(row, "x", 1), shifted(row, "x", 2), shifted(first_row, "x", 3)]
    square = shape((2, HW, HW))
    mine, other = local_call(column_kernel, (square, square), (at,), *rows, prefix, first)
    return mine, rotated(other, "c", 1)


def add(a, b):
    return (a.astype(f32) + b.astype(f32)).astype(bf)


def attended_blocks(offsets, me, q, keys, values, w, after=(), fetch=False):
    count = len(offsets)
    ids = jnp.stack([lax.rem(me + o + 8, 8) for o in offsets]).astype(jnp.int32)
    half = shape((RT, HALF))
    outs = local_call(
        functools.partial(attention_kernel, count), (half,) * (2 * count), (ids,),
        q, keys, values, *(() if fetch else (w,)), far=(w,) if fetch else (),
        flops=count * (5 << 29), after=after, mib=47 if fetch else 24,
        scratch=[
            pltpu.VMEM((2, G * RT, WINDOW), f32),
            pltpu.VMEM((2, G * RT, HW), f32),
            pltpu.VMEM((G * RT, 2 * HW), f32),
            pltpu.VMEM((count * RT, G * HW), bf),
        ] + ([pltpu.VMEM(w.shape, bf), pltpu.SemaphoreType.DMA] if fetch else []))
    return {o: outs[2 * t : 2 * t + 2] for t, o in enumerate(offsets)}


def reduced_rows(me, q, keys, values, w):
    part = attended_blocks((4,), me, q, keys, values, w, fetch=True)
    up = [rotated(part[4][0], "head", 1), None]
    down = [None, rotated(part[4][1], "head", -1)]
    sent, own = (), ()
    for k in (3, 2, 1):
        offsets = (k, -k, 0) if k == 2 else (k, -k)
        part = attended_blocks(offsets, me, q, keys, values, w, sent)
        own = part.get(0, ()) if k == 2 else own
        sent = []
        for n in range(2):
            ahead, back = part[k][n], part[-k][n]
            ahead = ahead if up[n] is None else add(up[n], ahead)
            back = back if down[n] is None else add(down[n], back)
            up[n] = rotated(ahead, "head", 1)
            down[n] = rotated(back, "head", -1)
            sent += [ahead, back]
    return (*up, *down, *own)


def delta_blocks(offsets, me, halves, weights, terms):
    count = len(offsets)
    ids = jnp.stack([lax.rem(me + o + 8, 8) for o in offsets]).astype(jnp.int32)
    return local_call(
        functools.partial(block_kernel, count),
        (shape((count, W4, HW)), shape((count, W4, HW), f32), shape((count, G, HW, 2 * HW))),
        (ids,), *halves, weights, *terms, flops=count * (5 << 29), mib=14)


def delta_rows(at, a, b, weights, terms):
    me = at[3]
    offsets = []
    parts = []
    weights = local_call(
        weights_kernel, shape((2 * HALF, 6 * HW)), (), far=weights, after=(a,), flops=3 << 30,
        mib=36, scratch=[pltpu.SemaphoreType.DMA((3,))])
    up, down = [a, b], [a, b]
    for k in (1, 2, 3):
        up = [rotated(h, "head", 1) for h in up]
        down = [rotated(h, "head", -1) for h in down]
        own = (a, b) if k == 1 else ()
        offsets.append((0, -k, k) if own else (-k, k))
        parts += delta_blocks(offsets[-1], me, (*own, *up, *down), weights, terms)
    last = (rotated(up[0], "head", 1), rotated(down[1], "head", -1))
    offsets.append((4,))
    parts += delta_blocks((4,), me, last, weights, terms)
    return local_call(
        functools.partial(chain_kernel, tuple(offsets)),
        (shape((2, HW, 2 * HW)),) * 2 + (shape((G, TOK, HW)), shape((TOK, G * HW), f32)),
        (at,), terms[1], *parts, mib=20,
        scratch=[
            pltpu.VMEM((8, W4, HW), bf),
            pltpu.VMEM((8, W4, HW), f32),
            pltpu.VMEM((8, G, HW, 2 * HW), bf),
        ])


def body(
    residual,
    sliding_query_heads,
    sliding_key_heads,
    sliding_value_heads,
    output_weight,
    norm_gain,
    query_weight,
    key_weight,
    value_weight,
    write_strength,
    log_decay,
):
    x, y, c, me = (lax.axis_index(a) for a in SEQ + ("head",))
    at = jnp.stack([x, y, c, me]).astype(jnp.int32)
    shard = (x * lax.axis_size("y") + y) * 2 + c
    low = jnp.maximum(0, (WINDOW // TOK - shard) * TOK).astype(jnp.int32)[None]
    own = local_call(
        join_kernel, shape((TOK, 2 * HW)), (),
        far=(sliding_key_heads, sliding_value_heads), scratch=[pltpu.SemaphoreType.DMA((2,))])
    d, odd = earlier_rows(own)
    weights = (query_weight, key_weight, value_weight)
    terms = decay_terms(write_strength, log_decay)
    wide = shape((9 * TOK, 2 * HW))
    keys, values = local_call(
        window_kernel, (wide, wide), (low,), far=(own, d[2], d[4], d[6], d[8], odd), mib=16,
        scratch=[pltpu.SemaphoreType.DMA((9, 2))])
    sums = reduced_rows(me, sliding_query_heads, keys, values, output_weight)
    half = shape((RT, HALF))
    mixed_stream, a, b = local_call(
        norm_kernel, (shape(residual.shape), half, half), (),
        *sums, residual, norm_gain[None, :])
    maps, theirs, twisted, local = delta_rows(at, a, b, weights, terms)
    mine, other = incoming_state(at, maps, theirs)
    delta_output = local_call(
        readout_kernel, shape((TOK, G * HW)), (at,), mine, other, twisted, local)
    return mixed_stream, delta_output


def solution(mesh):
    devices = mesh.devices.reshape(4, 4, 2, 8)
    split = Mesh(devices, SEQ + ("head",))
    in_specs = (
        P(SEQ + ("head",), None),
        P(SEQ, "head"),
        P(SEQ, "head"),
        P(SEQ, "head"),
        P("head", None),
        P(),
        P(None, "head"),
        P(None, "head"),
        P(None, "head"),
        P("head", SEQ),
        P("head", SEQ),
    )
    out_specs = (P(SEQ + ("head",), None), P(SEQ, "head"))
    return jax.shard_map(body, mesh=split, in_specs=in_specs, out_specs=out_specs, check_vma=False)
```
